32 devices in a mesh: groups: 2 (over y), tensor: 16 (over z, x, core).
Axes of the slice: x: 2, y: 2, z: 4, core: 2. Of those that a mesh axis runs over, the one named last changes fastest.
Arguments:
- normed_input: bfloat16 [16, 2, 8192], P('groups', None, 'tensor'), parts along dimension 0, may hold values from -6 to 6
- query_weight: bfloat16 [8192, 8192], P('tensor'), may hold values from -0.0625 to 0.0625
- query_gain: float32 [128], replicated, may hold values from 0.5 to 50
- image_cache: bfloat16 [32, 1601, 2048], P(('groups', 'tensor')), parts along dimension 0, may hold values from -18 to 18
- tile_count: int32 [16], P('groups'), parts along dimension 0, may hold values from 1 to 4, as said below
- image_first_slot: int32 [16], P('groups'), parts along dimension 0, may hold values from 0 to 15, as said below
- cross_tile_mask: int32 [16, 2, 4], P('groups'), parts along dimension 0, may hold values 0 or 1
- output_weight: bfloat16 [8192, 8192], P(None, 'tensor'), may hold values from -0.0625 to 0.0625
- output_gate: float32 [1], replicated, may hold values from 0.3 to 1.5
Outputs:
- cross_output: bfloat16 [16, 2, 8192], P('groups', None, 'tensor'), parts along dimension 0
The draws below stay inside these ranges and needn't reach their ends.
There are 2 independent parts, one for each index of `groups`. The reference program is written for one: setup_inputs(seed, part) draws one part's arguments, and reference() takes and returns one part's arrays. A program takes and returns all parts, laid end to end along the dimension named above; an argument that names none is the same for every part. Nothing has to cross between parts.
Inputs may be any that keep to these rules, and one draw needn't show every extreme that they name: tile_count sums to 16; some row has 4 tiles. Row r's tiles are pool slots image_first_slot[r] to image_first_slot[r] + tile_count[r] - 1; the images fill all 16 slots, each slot belonging to exactly one row.
All inputs are finite; a program needn't handle non-finite values.
Results may differ from the reference program's by a relative error of at most 0.0077.
Values may be sent and summed in bfloat16 or wider, within the bound.
No kernel may reach another device: no remote copies, remote signals or barrier semaphores. Data moves between devices by JAX's collectives and lax.ppermute only.
A program may use at most 64 MiB of HBM per device.

```python
import math
import jax
import jax.numpy as jnp
from jax import lax

D = 8192
QH = 64
KVH = 8
HD = 128
TILE_TOK = 1601
MAX_TILES = 4
STEPS = 2
ROWS = 8
SLOTS = 16


def tile_layout(key):
    layout_key = jax.random.fold_in(key, 71)
    patterns = jnp.array([[4, 2, 1, 1], [1, 4, 1, 2], [2, 1, 1, 4], [1, 1, 4, 2], [2, 2, 2, 2], [3, 3, 1, 1], [1, 3, 2, 2], [3, 1, 1, 3]], dtype=jnp.int32)
    picked = jax.random.randint(jax.random.fold_in(layout_key, 1), (ROWS // 4,), 0, 8)
    picked = picked.at[0].set(picked[0] % 4)
    counts = jnp.take(patterns, picked, axis=0).reshape(ROWS)
    shuffle = jax.random.permutation(jax.random.fold_in(layout_key, 2), ROWS)
    counts = counts[shuffle]
    placing = jax.random.permutation(jax.random.fold_in(layout_key, 3), ROWS)
    ordered = counts[placing]
    single = jnp.argmax((ordered == 1).astype(jnp.int32)).astype(jnp.int32)
    last_row = placing[ROWS - 1]
    single_row = placing[single]
    placing = placing.at[single].set(last_row).at[ROWS - 1].set(single_row)
    ordered = counts[placing]
    starts_ordered = (jnp.cumsum(ordered) - ordered).astype(jnp.int32)
    starts = jnp.zeros((ROWS,), jnp.int32).at[placing].set(starts_ordered)
    return (counts.astype(jnp.int32), starts)


def draw_tile_count(key, part):
    return tile_layout(key)[0]


def draw_image_first_slot(key, part):
    return tile_layout(key)[1]


def draw_query_gain(key, part):
    gains = jnp.exp(jax.random.uniform(key, (HD,), minval=math.log(0.5), maxval=math.log(3.0)))
    return gains.astype(jnp.float32)


def draw_image_cache(key, part):
    key_keys, key_scale, key_values = jax.random.split(key, 3)
    width = KVH * HD
    token_scale = jnp.exp(jax.random.uniform(key_scale, (SLOTS, TILE_TOK, 1), minval=math.log(0.3), maxval=math.log(3.0)))
    keys = jnp.clip(jax.random.normal(key_keys, (SLOTS, TILE_TOK, width)), -6.0, 6.0) * token_scale
    values = 2.0 * jnp.clip(jax.random.normal(key_values, (SLOTS, TILE_TOK, width)), -6.0, 6.0)
    return jnp.concatenate([keys, values], axis=-1).astype(jnp.bfloat16)


def touch_ends(values, key, least, largest):
    longest = values.shape.index(max(values.shape))
    spots = []
    for shift in (0, 1):
        where = [jax.random.randint(jax.random.fold_in(key, axis), (), 0, length) for axis, length in enumerate(values.shape)]
        where[longest] = (where[longest] + shift) % values.shape[longest]
        spots.append(tuple(where))
    return values.at[spots[0]].set(least).at[spots[1]].set(largest)


def block_levels(stream_key, shape, cuts, least, largest):
    def one(axis_at, blocks):
        draws = jax.random.uniform(jax.random.fold_in(jax.random.fold_in(stream_key, 6), axis_at), (blocks,), jnp.float32, least / len(cuts), largest / len(cuts))
        return jnp.repeat(jnp.exp(draws), shape[axis_at] // blocks).reshape((-1,) + (1,) * (len(shape) - axis_at - 1))

    loudness = one(*cuts[0])
    for cut in cuts[1:]:
        loudness = loudness * one(*cut)
    return loudness


def scatter_about(stream_key, extent, deviation, bound, shards=(), kind=jnp.bfloat16):
    values = deviation * jax.random.normal(stream_key, extent, jnp.float32)
    if shards:
        values = values * block_levels(stream_key, extent, shards, -0.22, 0.18)
    return jnp.clip(values, -bound, bound).astype(kind)


def setup_inputs(seed: int = 0, part: int = 0) -> dict:
    arg_keys = jax.random.split(jax.random.key(seed), 10)
    part_keys = jax.random.split(jax.random.fold_in(arg_keys[9], part), 10)
    return {
        "normed_input": scatter_about(part_keys[0], (ROWS, STEPS, D), 1.0, 6.0, ((2, 16),)),
        "query_weight": scatter_about(arg_keys[1], (D, QH * HD), D ** -0.5, 0.0625, ((0, 16),)),
        "query_gain": draw_query_gain(jax.random.fold_in(arg_keys[9], 71), part),
        "image_cache": draw_image_cache(jax.random.fold_in(jax.random.fold_in(arg_keys[9], part), 71), part),
        "tile_count": draw_tile_count(jax.random.fold_in(jax.random.fold_in(arg_keys[9], part), 71), part),
        "image_first_slot": draw_image_first_slot(jax.random.fold_in(jax.random.fold_in(arg_keys[9], part), 71), part),
        "cross_tile_mask": touch_ends((jax.random.randint(part_keys[6], (ROWS, STEPS, MAX_TILES), 0, 2) < 1).astype(jnp.int32), jax.random.fold_in(part_keys[6], 1), 0, 1),
        "output_weight": scatter_about(arg_keys[7], (QH * HD, D), (QH * HD) ** -0.5, 0.0625, ((1, 16),)),
        "output_gate": jnp.clip(jax.random.uniform(arg_keys[8], (1,), jnp.float32, 0.3, 1.5), 0.3, 1.5),
    }


EPSILON = 1e-05
NEGATIVE_FLOOR = -1e+30

def membership(image_first_slot, tile_count, pool_slots):
    ends = image_first_slot + tile_count
    return (pool_slots[:, None] >= image_first_slot[None, :]) & (pool_slots[:, None] < ends[None, :])

def active_status(member_flag, image_first_slot, cross_tile_mask, pool_slots):
    member_int = member_flag.astype(jnp.int32)
    tile_index = lax.optimization_barrier(jnp.sum(member_int * (pool_slots[:, None] - image_first_slot[None, :]), axis=1))
    row_masks = lax.optimization_barrier(jnp.sum(member_int[:, :, None, None] * cross_tile_mask[None], axis=1))
    positions = jnp.arange(cross_tile_mask.shape[2], dtype=jnp.int32)
    chosen = lax.optimization_barrier(jnp.sum(jnp.where(positions[None, None, :] == tile_index[:, None, None], row_masks, 0), axis=2))
    return (tile_index[:, None] == 0) | (chosen == 1)

def tile_partial(query_rows, cache_tile):
    steps = query_rows.shape[0]
    kv_width = cache_tile.shape[1] // 2
    kv_heads = kv_width // HD
    group = query_rows.shape[1] // kv_width
    grouped = query_rows.reshape(steps, kv_heads, group, HD).astype(jnp.float32)
    keys = cache_tile[:, :kv_width].reshape(-1, kv_heads, HD).astype(jnp.float32)
    values = cache_tile[:, kv_width:].reshape(-1, kv_heads, HD).astype(jnp.float32)
    scores = jnp.einsum('skgd,tkd->skgt', grouped, keys) * (1.0 / math.sqrt(HD))
    tops = lax.optimization_barrier(jnp.max(scores, axis=3))
    weights = jnp.exp(scores - tops[..., None]).astype(jnp.bfloat16).astype(jnp.float32)
    totals = lax.optimization_barrier(jnp.sum(weights, axis=3))
    mixed = jnp.einsum('skgt,tkd->skgd', weights, values)
    return (tops.reshape(steps, -1), totals.reshape(steps, -1), mixed.reshape(steps, -1))

def slot_term(operands):
    return tile_partial(operands[0], operands[1])

def reference(normed_input, query_weight, query_gain, image_cache, tile_count, image_first_slot, cross_tile_mask, output_weight, output_gate):
    flattened = normed_input.reshape(ROWS * STEPS, D)
    query = jnp.dot(flattened, query_weight, preferred_element_type=jnp.float32)
    heads = query.reshape(ROWS * STEPS, QH, HD)
    normed = heads * lax.rsqrt(lax.optimization_barrier(jnp.mean(heads * heads, axis=2, keepdims=True)) + EPSILON) * query_gain
    normed = normed.astype(jnp.bfloat16).reshape(ROWS, STEPS * QH * HD)
    pool_slots = jnp.arange(SLOTS, dtype=jnp.int32)
    member_flag = membership(image_first_slot, tile_count, pool_slots)
    active_entry = active_status(member_flag, image_first_slot, cross_tile_mask, pool_slots)
    selected = jnp.dot(member_flag.astype(jnp.bfloat16), normed, preferred_element_type=jnp.float32)
    selected = selected.astype(jnp.bfloat16).reshape(SLOTS, STEPS, QH * HD)
    tops, totals, mixed = lax.map(slot_term, (selected, image_cache))
    masked = jnp.where(active_entry[:, :, None], tops, NEGATIVE_FLOOR)
    row_max = lax.optimization_barrier(jnp.max(jnp.where(member_flag[:, :, None, None], masked[:, None], NEGATIVE_FLOOR), axis=0))
    slot_max = lax.optimization_barrier(jnp.max(jnp.where(member_flag[:, :, None, None], row_max[None], NEGATIVE_FLOOR), axis=1))
    factor = jnp.where(active_entry[:, :, None], jnp.exp(masked - slot_max), 0.0)
    numer = (mixed.reshape(SLOTS, STEPS, QH, HD) * factor[..., None]).reshape(SLOTS, STEPS * QH * HD)
    denom = (totals * factor).reshape(SLOTS, STEPS * QH)
    member_float = member_flag.astype(jnp.float32).T
    numer_rows = jnp.dot(member_float, numer, precision=lax.Precision.HIGHEST).reshape(ROWS * STEPS, QH, HD)
    denom_rows = jnp.dot(member_float, denom, precision=lax.Precision.HIGHEST).reshape(ROWS * STEPS, QH)
    attended = (numer_rows / denom_rows[..., None]).astype(jnp.bfloat16).reshape(ROWS * STEPS, QH * HD)
    projected = jnp.dot(attended, output_weight, preferred_element_type=jnp.float32)
    result = jnp.tanh(output_gate[0]) * projected
    return result.astype(jnp.bfloat16).reshape(ROWS, STEPS, D)
```

```python
import functools
import math

import jax
import jax.numpy as jnp
from jax import lax
from jax.experimental import pallas as pl
from jax.experimental.pallas import tpu as pltpu
from jax.sharding import PartitionSpec as P

EPSILON = 1e-05
NEGATIVE_FLOOR = -1e30
AXIS = "tensor"
F32 = jnp.float32
BF16 = jnp.bfloat16
VMEM = pl.BlockSpec(memory_space=pltpu.VMEM)
SMEM = pl.BlockSpec(memory_space=pltpu.SMEM)
ANY = pl.BlockSpec(memory_space=pl.ANY)


def struct(shape, dtype):
    return jax.ShapeDtypeStruct(shape, dtype)


def params(mebibytes):
    return pltpu.CompilerParams(vmem_limit_bytes=mebibytes << 20)


def scatter_stages(bits):
    if bits < 3:
        return [[bit] for bit in range(bits)]
    return [[0], [1, 2]] + [[bit] for bit in range(3, bits)]


def offsets(group):
    result = [0]
    for bit in group:
        result = result + [other | (1 << bit) for other in result]
    return result


def positions(stages):
    result = [0]
    for group in stages:
        result = [base | step for base in result for step in offsets(group)]
    return result


def move_bits(value, moves):
    result = value & 0
    for source, target in moves:
        result = result | (((value >> source) & 1) << target)
    return result


def exchange(array, difference, count):
    return lax.ppermute(array, AXIS, [(i, i ^ difference) for i in range(count)])


def project_kernel(
    order, chunks, kv_heads, group, head_size, x_ref, weight_hbm, first_ref, count_ref, keep_ref,
    send_ref, weight, sems
):
    rows, steps, depth = x_ref.shape
    width = weight.shape[1]
    chunk = width // chunks
    copies = [
        pltpu.make_async_copy(
            weight_hbm.at[:, pl.ds(c * chunk, chunk)], weight.at[:, pl.ds(c * chunk, chunk)], sems.at[c]
        )
        for c in range(chunks)
    ]
    for copy in copies:
        copy.start()
    slots = len(order)
    half = slots // 2
    me = lax.axis_index(AXIS)
    shape = (steps * slots, rows * steps)
    out_row = lax.broadcasted_iota(jnp.int32, shape, 0)
    place = out_row % slots
    step = out_row // slots
    in_row = lax.broadcasted_iota(jnp.int32, shape, 1)
    bits = range(slots.bit_length() - 1)
    slot = move_bits(place, [(i, order[1 << i].bit_length() - 1) for i in bits]) ^ me
    start = jnp.zeros(shape, jnp.int32)
    length = jnp.zeros(shape, jnp.int32)
    for row in range(rows):
        here = in_row // steps == row
        start = jnp.where(here, first_ref[row], start)
        length = jnp.where(here, count_ref[row], length)
    chosen = (slot >= start) & (slot < start + length) & (in_row % steps == step)
    flat = x_ref[...].reshape(rows * steps, depth)
    picked = jnp.dot(
        jnp.where(chosen, 1.0, 0.0).astype(BF16), flat, preferred_element_type=F32
    ).astype(BF16)
    tile_rows = steps * kv_heads * group
    heads_per_chunk = chunk // head_size
    for c in range(chunks):
        copies[c].wait()
        result = jnp.dot(
            picked, weight[:, c * chunk : (c + 1) * chunk], preferred_element_type=F32
        )
        for local in range(heads_per_chunk):
            head = c * heads_per_chunk + local
            for s in range(steps):
                at = (head // group) * steps * group + s * group + head % group
                block = result[s * slots : (s + 1) * slots, local * head_size : (local + 1) * head_size]
                keep_ref[pl.ds(at, half, stride=tile_rows), :] = block[:half]
                send_ref[pl.ds(at, half, stride=tile_rows), :] = block[half:]


def sum_kernel(inputs, *refs):
    total = refs[0][...]
    for ref in refs[1:inputs]:
        total = total + ref[...]
    outs = refs[inputs:]
    size = outs[0].shape[0]
    for i, out in enumerate(outs):
        out[...] = total[i * size : (i + 1) * size]


def add_and_split(arrays, pieces):
    rows, lanes = arrays[0].shape
    return pl.pallas_call(
        functools.partial(sum_kernel, len(arrays)),
        out_shape=[struct((rows // pieces, lanes), F32)] * pieces,
        in_specs=[VMEM] * len(arrays),
        out_specs=[VMEM] * pieces,
        compiler_params=params(16),
    )(*arrays)


def attend_kernel(
    partials, kv_heads, group, steps, *refs
):
    parts = refs[:partials]
    gain_ref, cache_ref, first_ref, count_ref, mask_ref, out_ref = refs[partials:]
    head_size = gain_ref.shape[-1]
    kv_width = kv_heads * head_size
    query = parts[0][...]
    for part in parts[1:]:
        query = query + part[...]
    mean = jnp.mean(query * query, axis=1, keepdims=True)
    normed = (query * lax.rsqrt(mean + EPSILON) * gain_ref[...]).astype(BF16)
    me = lax.axis_index(AXIS)
    rows = first_ref.shape[0]

    def find(row, carry):
        owner, tile = carry
        offset = me - first_ref[row]
        inside = (offset >= 0) & (offset < count_ref[row])
        return jnp.where(inside, row, owner), jnp.where(inside, offset, tile)

    owner, tile = lax.fori_loop(0, rows, find, (jnp.int32(0), jnp.int32(0)), unroll=rows <= 16)
    size = steps * group
    row_in_tile = lax.broadcasted_iota(jnp.int32, (size, head_size), 0)
    lane = lax.broadcasted_iota(jnp.int32, (size, head_size), 1)
    stats = jnp.zeros((size, head_size), F32)
    scale = 1.0 / math.sqrt(head_size)
    for h in range(kv_heads):
        keys = cache_ref[0, :, h * head_size : (h + 1) * head_size]
        values = cache_ref[0, :, kv_width + h * head_size : kv_width + (h + 1) * head_size]
        scores = lax.dot_general(
            normed[h * size : (h + 1) * size],
            keys,
            (((1,), (1,)), ((), ())),
            preferred_element_type=F32,
        ) * scale
        top = jnp.max(scores, axis=1, keepdims=True)
        weights = jnp.exp(scores - top).astype(BF16)
        total = jnp.sum(weights.astype(F32), axis=1, keepdims=True)
        mixed = jnp.dot(weights, values, preferred_element_type=F32)
        out_ref[h * size : (h + 1) * size, :] = (mixed / total).astype(BF16)
        here = lane % kv_heads == h
        stats = jnp.where(here, jnp.where(lane < 3 * kv_heads, top, total), stats)
    live = jnp.zeros((size, head_size), jnp.bool_)
    for s in range(steps):
        alive = (tile == 0) | (mask_ref[owner, s, tile] == 1)
        live = live | ((row_in_tile // group == s) & alive)
    stats = jnp.where(live | (lane >= 3 * kv_heads), stats, NEGATIVE_FLOOR)
    high = stats.astype(BF16).astype(F32)
    rest = stats - high
    middle = rest.astype(BF16).astype(F32)
    low = rest - middle
    piece = (lane // kv_heads) % 3
    packed = jnp.where(piece == 0, high, jnp.where(piece == 1, middle, low))
    out_ref[kv_heads * size :, :] = packed.astype(BF16)


def finish_kernel(
    order, kv_heads, group, steps, max_tiles, gate_ref, first_ref, count_ref, tiles_ref, weight_ref, out_ref, stats, turned
):
    rows = first_ref.shape[0]
    head_size = tiles_ref.shape[-1]
    size = steps * group
    block = (kv_heads + 1) * size
    slots = tiles_ref.shape[0]
    me = lax.axis_index(AXIS)
    packed = tiles_ref[:, kv_heads * size :, :].astype(F32).reshape(slots * size, head_size)
    whole = (
        packed
        + pltpu.roll(packed, head_size - kv_heads, 1)
        + pltpu.roll(packed, head_size - 2 * kv_heads, 1)
    )
    stats[0] = whole
    stats[1] = pltpu.roll(whole, head_size - 3 * kv_heads, 1)
    pairs = rows * steps
    moves = [(order[1 << i].bit_length() - 1, i) for i in range(slots.bit_length() - 1)]

    def one_row(row, carry):
        begin = first_ref[row]
        length = count_ref[row]
        places = [
            move_bits(me ^ (begin + jnp.minimum(k, length - 1)), moves) for k in range(max_tiles)
        ]
        tops = []
        for k in range(max_tiles):
            top = stats[0, pl.ds(places[k] * size, size), :]
            tops.append(jnp.where(k < length, top, NEGATIVE_FLOOR))
        best = functools.reduce(jnp.maximum, tops)
        factors = []
        for k in range(max_tiles):
            total = stats[1, pl.ds(places[k] * size, size), :]
            factor = jnp.exp(tops[k] - best) * total
            factors.append(jnp.where(tops[k] > 0.5 * NEGATIVE_FLOOR, factor, 0.0))
        denominator = functools.reduce(jnp.add, factors)
        shares = [factor / denominator for factor in factors]
        for h in range(kv_heads):
            mixed = jnp.zeros((size, head_size), F32)
            for k in range(max_tiles):
                value = tiles_ref[places[k], h * size : (h + 1) * size, :].astype(F32)
                mixed = mixed + shares[k][:, h : h + 1] * value
            for s in range(steps):
                turned[pl.ds(h * group * pairs + row * steps + s, group, stride=pairs), :] = mixed[
                    s * group : (s + 1) * group
                ]
        return carry

    lax.fori_loop(0, rows, one_row, 0)
    total = jnp.zeros((pairs, weight_ref.shape[1]), F32)
    for h in range(kv_heads):
        left = jnp.concatenate(
            [
                turned[(h * group + g) * pairs : (h * group + g + 1) * pairs, :].astype(BF16)
                for g in range(group)
            ],
            axis=1,
        )
        span = group * head_size
        total = total + jnp.dot(
            left, weight_ref[h * span : (h + 1) * span, :], preferred_element_type=F32
        )
    gate = jnp.tanh(jnp.full((1, 1), gate_ref[0], F32))
    result = (total * gate).astype(BF16)
    out_ref[...] = result.reshape(rows, steps, result.shape[1])


def body(
    devices,
    normed_input,
    query_weight,
    query_gain,
    image_cache,
    tile_count,
    image_first_slot,
    cross_tile_mask,
    output_weight,
    output_gate,
):
    rows, steps, depth = normed_input.shape
    head_size = query_gain.shape[0]
    width = query_weight.shape[1]
    heads = width // head_size
    kv_heads = image_cache.shape[2] // (2 * head_size)
    group = heads // kv_heads
    tile_rows = steps * heads
    stages = scatter_stages(devices.bit_length() - 1)
    order = positions(stages)
    half = devices // 2
    chunks = 8
    keep, send = pl.pallas_call(
        functools.partial(project_kernel, order, chunks, kv_heads, group, head_size),
        out_shape=[struct((half * tile_rows, head_size), F32)] * 2,
        in_specs=[VMEM, ANY, SMEM, SMEM],
        out_specs=[VMEM, VMEM],
        scratch_shapes=[pltpu.VMEM((depth, width), BF16), pltpu.SemaphoreType.DMA((chunks,))],
        compiler_params=params(40),
    )(normed_input, query_weight, image_first_slot, tile_count)
    parts = [keep, exchange(send, 1, devices)]
    for group_bits in stages[1:]:
        steps_out = offsets(group_bits)
        pieces = add_and_split(parts, len(steps_out))
        parts = [pieces[0]] + [
            exchange(piece, step, devices) for piece, step in zip(pieces[1:], steps_out[1:])
        ]
    block = (kv_heads + 1) * steps * group
    tile = pl.pallas_call(
        functools.partial(attend_kernel, len(parts), kv_heads, group, steps),
        out_shape=struct((block, head_size), BF16),
        in_specs=[VMEM] * (len(parts) + 2) + [SMEM] * 3,
        out_specs=VMEM,
        compiler_params=params(16),
    )(*parts, query_gain, image_cache, image_first_slot, tile_count, cross_tile_mask)
    gathered = tile[None]
    for group_bits in reversed(stages):
        gathered = jnp.concatenate(
            [gathered] + [exchange(gathered, step, devices) for step in offsets(group_bits)[1:]], axis=0
        )
    return pl.pallas_call(
        functools.partial(finish_kernel, order, kv_heads, group, steps, cross_tile_mask.shape[2]),
        out_shape=struct((rows, steps, output_weight.shape[1]), BF16),
        in_specs=[SMEM] * 3 + [VMEM, VMEM],
        out_specs=VMEM,
        scratch_shapes=[
            pltpu.VMEM((2, devices * steps * group, head_size), F32),
            pltpu.VMEM((heads * rows * steps, head_size), F32),
        ],
        compiler_params=params(24),
    )(output_gate, image_first_slot, tile_count, gathered, output_weight)


def solution(mesh):
    return jax.shard_map(
        functools.partial(body, mesh.shape[AXIS]),
        mesh=mesh,
        in_specs=(
            P("groups", None, "tensor"),
            P("tensor", None),
            P(),
            P(("groups", "tensor"), None, None),
            P("groups"),
            P("groups"),
            P("groups", None, None),
            P(None, "tensor"),
            P(),
        ),
        out_specs=P("groups", None, "tensor"),
        check_vma=False,
    )
```

```python
import functools
import math

import jax
import jax.numpy as jnp
from jax import lax
from jax.experimental import pallas as pl
from jax.experimental.pallas import tpu as pltpu
from jax.sharding import PartitionSpec as P

EPSILON = 1e-05
NEGATIVE_FLOOR = -1e30
AXIS = "tensor"
F32 = jnp.float32
BF16 = jnp.bfloat16
VMEM = pl.BlockSpec(memory_space=pltpu.VMEM)
SMEM = pl.BlockSpec(memory_space=pltpu.SMEM)
ANY = pl.BlockSpec(memory_space=pl.ANY)
HBM = pl.BlockSpec(memory_space=pltpu.HBM)


def struct(shape, dtype):
    return jax.ShapeDtypeStruct(shape, dtype)


def in_hbm(array):
    return pltpu.with_memory_space_constraint(array, pltpu.HBM)


def params(mebibytes):
    return pltpu.CompilerParams(vmem_limit_bytes=mebibytes << 20)


def scatter_stages(bits):
    if bits < 3:
        return [[bit] for bit in range(bits)]
    return [[0], [1, 2]] + [[bit] for bit in range(3, bits)]


def offsets(group):
    result = [0]
    for bit in group:
        result = result + [other | (1 << bit) for other in result]
    return result


def positions(stages):
    result = [0]
    for group in stages:
        result = [base | step for base in result for step in offsets(group)]
    return result


def move_bits(value, moves):
    result = value & 0
    for source, target in moves:
        result = result | (((value >> source) & 1) << target)
    return result


def exchange(array, difference, count):
    return lax.ppermute(array, AXIS, [(i, i ^ difference) for i in range(count)])


def project_kernel(
    order, chunks, kv_heads, group, head_size, x_hbm, weight_hbm, first_hbm, count_hbm, keep_ref,
    send_ref, weight, x_ref, first_ref, count_ref, sems, small_sems
):
    rows, steps, depth = x_ref.shape
    width = weight.shape[1]
    chunk = width // chunks
    small = [
        pltpu.make_async_copy(source, target, small_sems.at[i])
        for i, (source, target) in enumerate(
            [(x_hbm, x_ref), (first_hbm, first_ref), (count_hbm, count_ref)]
        )
    ]
    for copy in small:
        copy.start()
    copies = [
        pltpu.make_async_copy(
            weight_hbm.at[:, pl.ds(c * chunk, chunk)], weight.at[:, pl.ds(c * chunk, chunk)], sems.at[c]
        )
        for c in range(chunks)
    ]
    for copy in copies:
        copy.start()
    for copy in small:
        copy.wait()
    slots = len(order)
    half = slots // 2
    me = lax.axis_index(AXIS)
    shape = (steps * slots, rows * steps)
    out_row = lax.broadcasted_iota(jnp.int32, shape, 0)
    place = out_row % slots
    step = out_row // slots
    in_row = lax.broadcasted_iota(jnp.int32, shape, 1)
    bits = range(slots.bit_length() - 1)
    slot = move_bits(place, [(i, order[1 << i].bit_length() - 1) for i in bits]) ^ me
    start = jnp.zeros(shape, jnp.int32)
    length = jnp.zeros(shape, jnp.int32)
    for row in range(rows):
        here = in_row // steps == row
        start = jnp.where(here, first_ref[row], start)
        length = jnp.where(here, count_ref[row], length)
    chosen = (slot >= start) & (slot < start + length) & (in_row % steps == step)
    flat = x_ref[...].reshape(rows * steps, depth)
    picked = jnp.dot(
        jnp.where(chosen, 1.0, 0.0).astype(BF16), flat, preferred_element_type=F32
    ).astype(BF16)
    tile_rows = steps * kv_heads * group
    heads_per_chunk = chunk // head_size
    for c in range(chunks):
        copies[c].wait()
        result = jnp.dot(
            picked, weight[:, c * chunk : (c + 1) * chunk], preferred_element_type=F32
        )
        for local in range(heads_per_chunk):
            head = c * heads_per_chunk + local
            for s in range(steps):
                at = (head // group) * steps * group + s * group + head % group
                block = result[s * slots : (s + 1) * slots, local * head_size : (local + 1) * head_size]
                keep_ref[pl.ds(at, half, stride=tile_rows), :] = block[:half]
                send_ref[pl.ds(at, half, stride=tile_rows), :] = block[half:]


def fetch_kernel(cache_hbm, after_ref, cache_ref, sems):
    del after_ref
    pieces = sems.shape[0]
    span = cache_hbm.shape[2] // pieces
    copies = [
        pltpu.make_async_copy(
            cache_hbm.at[:, :, pl.ds(i * span, span)], cache_ref.at[:, :, pl.ds(i * span, span)], sems.at[i]
        )
        for i in range(pieces)
    ]
    for copy in copies:
        copy.start()
    for copy in copies:
        copy.wait()


def fetch(cache, after):
    return pl.pallas_call(
        fetch_kernel,
        out_shape=struct(cache.shape, cache.dtype),
        in_specs=[HBM, ANY],
        out_specs=VMEM,
        scratch_shapes=[pltpu.SemaphoreType.DMA((4,))],
        compiler_params=params(1),
        cost_estimate=pl.CostEstimate(flops=0, bytes_accessed=2 * cache.size, transcendentals=0),
    )(in_hbm(cache), after)


def attend_kernel(
    kv_heads, group, steps, query_ref, gain_ref, cache_ref, first_ref, count_ref, mask_ref, out_ref
):
    head_size = gain_ref.shape[-1]
    kv_width = kv_heads * head_size
    join = 2 if kv_heads % 2 == 0 else 1
    span = join * head_size
    query = query_ref[...]
    mean = jnp.mean(query * query, axis=1, keepdims=True)
    normed = (query * lax.rsqrt(mean + EPSILON) * gain_ref[...]).astype(BF16)
    me = lax.axis_index(AXIS)
    rows = first_ref.shape[0]

    def find(row, carry):
        owner, tile = carry
        offset = me - first_ref[row]
        inside = (offset >= 0) & (offset < count_ref[row])
        return jnp.where(inside, row, owner), jnp.where(inside, offset, tile)

    owner, tile = lax.fori_loop(0, rows, find, (jnp.int32(0), jnp.int32(0)), unroll=rows <= 16)
    size = steps * group
    row_in_tile = lax.broadcasted_iota(jnp.int32, (size, head_size), 0)
    lane = lax.broadcasted_iota(jnp.int32, (size, head_size), 1)
    stats = jnp.zeros((size, head_size), F32)
    scale = 1.0 / math.sqrt(head_size)
    blank = jnp.zeros((size, head_size), BF16)
    for base in range(0, kv_heads, join):
        at = base * head_size
        keys = cache_ref[0, :, at : at + span]
        left = jnp.concatenate(
            [
                jnp.concatenate(
                    [
                        normed[(base + i) * size : (base + i + 1) * size] if i == j else blank
                        for j in range(join)
                    ],
                    axis=1,
                )
                for i in range(join)
            ],
            axis=0,
        )
        scores = lax.dot_general(
            left, keys, (((1,), (1,)), ((), ())), preferred_element_type=F32
        ) * scale
        top = jnp.max(scores, axis=1, keepdims=True)
        weights = jnp.exp(scores - top).astype(BF16)
        total = jnp.sum(weights.astype(F32), axis=1, keepdims=True)
        values = cache_ref[0, :, kv_width + at : kv_width + at + span]
        mixed = jnp.dot(weights, values, preferred_element_type=F32) / total
        for i in range(join):
            h = base + i
            rows_here = slice(i * size, (i + 1) * size)
            out_ref[h * size : (h + 1) * size, :] = mixed[
                rows_here, i * head_size : (i + 1) * head_size
            ].astype(BF16)
            here = lane % kv_heads == h
            stats = jnp.where(
                here, jnp.where(lane < 3 * kv_heads, top[rows_here], total[rows_here]), stats
            )
    live = jnp.zeros((size, head_size), jnp.bool_)
    for s in range(steps):
        alive = (tile == 0) | (mask_ref[owner, s, tile] == 1)
        live = live | ((row_in_tile // group == s) & alive)
    stats = jnp.where(live | (lane >= 3 * kv_heads), stats, NEGATIVE_FLOOR)
    high = stats.astype(BF16).astype(F32)
    rest = stats - high
    middle = rest.astype(BF16).astype(F32)
    low = rest - middle
    piece = (lane // kv_heads) % 3
    packed = jnp.where(piece == 0, high, jnp.where(piece == 1, middle, low))
    out_ref[kv_heads * size :, :] = packed.astype(BF16)


def finish_kernel(
    order, kv_heads, group, steps, max_tiles, gate_ref, first_ref, count_ref, tiles_ref, weight_ref, out_ref, stats, turned
):
    rows = first_ref.shape[0]
    head_size = tiles_ref.shape[-1]
    size = steps * group
    block = (kv_heads + 1) * size
    slots = tiles_ref.shape[0]
    me = lax.axis_index(AXIS)
    packed = tiles_ref[:, kv_heads * size :, :].astype(F32).reshape(slots * size, head_size)
    whole = (
        packed
        + pltpu.roll(packed, head_size - kv_heads, 1)
        + pltpu.roll(packed, head_size - 2 * kv_heads, 1)
    )
    stats[0] = whole
    stats[1] = pltpu.roll(whole, head_size - 3 * kv_heads, 1)
    pairs = rows * steps
    moves = [(order[1 << i].bit_length() - 1, i) for i in range(slots.bit_length() - 1)]

    def one_row(row, carry):
        begin = first_ref[row]
        length = count_ref[row]
        places = [
            move_bits(me ^ (begin + jnp.minimum(k, length - 1)), moves) for k in range(max_tiles)
        ]
        tops = []
        for k in range(max_tiles):
            top = stats[0, pl.ds(places[k] * size, size), :]
            tops.append(jnp.where(k < length, top, NEGATIVE_FLOOR))
        best = functools.reduce(jnp.maximum, tops)
        factors = []
        for k in range(max_tiles):
            total = stats[1, pl.ds(places[k] * size, size), :]
            factor = jnp.exp(tops[k] - best) * total
            factors.append(jnp.where(tops[k] > 0.5 * NEGATIVE_FLOOR, factor, 0.0))
        denominator = functools.reduce(jnp.add, factors)
        shares = [factor / denominator for factor in factors]
        for h in range(kv_heads):
            mixed = jnp.zeros((size, head_size), F32)
            for k in range(max_tiles):
                value = tiles_ref[places[k], h * size : (h + 1) * size, :].astype(F32)
                mixed = mixed + shares[k][:, h : h + 1] * value
            for s in range(steps):
                turned[pl.ds(h * group * pairs + row * steps + s, group, stride=pairs), :] = mixed[
                    s * group : (s + 1) * group
                ]
        return carry

    lax.fori_loop(0, rows, one_row, 0)
    total = jnp.zeros((pairs, weight_ref.shape[1]), F32)
    for h in range(kv_heads):
        left = jnp.concatenate(
            [
                turned[(h * group + g) * pairs : (h * group + g + 1) * pairs, :].astype(BF16)
                for g in range(group)
            ],
            axis=1,
        )
        span = group * head_size
        total = total + jnp.dot(
            left, weight_ref[h * span : (h + 1) * span, :], preferred_element_type=F32
        )
    gate = jnp.tanh(jnp.full((1, 1), gate_ref[0], F32))
    result = (total * gate).astype(BF16)
    out_ref[...] = result.reshape(rows, steps, result.shape[1])


def body(
    devices,
    normed_input,
    query_weight,
    query_gain,
    image_cache,
    tile_count,
    image_first_slot,
    cross_tile_mask,
    output_weight,
    output_gate,
):
    rows, steps, depth = normed_input.shape
    head_size = query_gain.shape[0]
    width = query_weight.shape[1]
    heads = width // head_size
    kv_heads = image_cache.shape[2] // (2 * head_size)
    group = heads // kv_heads
    tile_rows = steps * heads
    stages = scatter_stages(devices.bit_length() - 1)
    order = positions(stages)
    half = devices // 2
    chunks = 8
    keep, send = pl.pallas_call(
        functools.partial(project_kernel, order, chunks, kv_heads, group, head_size),
        out_shape=[struct((half * tile_rows, head_size), F32)] * 2,
        in_specs=[HBM] * 4,
        out_specs=[VMEM, VMEM],
        scratch_shapes=[
            pltpu.VMEM((depth, width), BF16),
            pltpu.VMEM(normed_input.shape, BF16),
            pltpu.SMEM(image_first_slot.shape, jnp.int32),
            pltpu.SMEM(tile_count.shape, jnp.int32),
            pltpu.SemaphoreType.DMA((chunks,)),
            pltpu.SemaphoreType.DMA((3,)),
        ],
        compiler_params=params(12),
    )(*[in_hbm(x) for x in (normed_input, query_weight, image_first_slot, tile_count)])
    total = keep + exchange(send, 1, devices)
    cache = None
    for group_bits in stages[1:]:
        steps_out = offsets(group_bits)
        size = total.shape[0] // len(steps_out)
        pieces = [total[i * size : (i + 1) * size] for i in range(len(steps_out))]
        sent = [piece.astype(jnp.float16) for piece in pieces[1:]]
        got = [exchange(piece, step, devices) for piece, step in zip(sent, steps_out[1:])]
        if cache is None:
            cache = fetch(image_cache, pieces[0])
        total = functools.reduce(jnp.add, [pieces[0]] + [piece.astype(F32) for piece in got])
    block = (kv_heads + 1) * steps * group
    tile = pl.pallas_call(
        functools.partial(attend_kernel, kv_heads, group, steps),
        out_shape=struct((block, head_size), BF16),
        in_specs=[VMEM] * 3 + [SMEM] * 3,
        out_specs=VMEM,
        compiler_params=params(6),
    )(total, query_gain, cache, image_first_slot, tile_count, cross_tile_mask)
    gathered = tile[None]
    for group_bits in reversed(stages):
        gathered = jnp.concatenate(
            [gathered] + [exchange(gathered, step, devices) for step in offsets(group_bits)[1:]], axis=0
        )
    return pl.pallas_call(
        functools.partial(finish_kernel, order, kv_heads, group, steps, cross_tile_mask.shape[2]),
        out_shape=struct((rows, steps, output_weight.shape[1]), BF16),
        in_specs=[SMEM] * 3 + [VMEM, VMEM],
        out_specs=VMEM,
        scratch_shapes=[
            pltpu.VMEM((2, devices * steps * group, head_size), F32),
            pltpu.VMEM((heads * rows * steps, head_size), F32),
        ],
        compiler_params=params(8),
    )(output_gate, image_first_slot, tile_count, gathered, output_weight)


def solution(mesh):
    return jax.shard_map(
        functools.partial(body, mesh.shape[AXIS]),
        mesh=mesh,
        in_specs=(
            P("groups", None, "tensor"),
            P("tensor", None),
            P(),
            P(("groups", "tensor"), None, None),
            P("groups"),
            P("groups"),
            P("groups", None, None),
            P(None, "tensor"),
            P(),
        ),
        out_specs=P("groups", None, "tensor"),
        check_vma=False,
    )
```

```python
import functools
import math

import jax
import jax.numpy as jnp
from jax import lax
from jax.experimental import pallas as pl
from jax.experimental.pallas import tpu as pltpu
from jax.sharding import PartitionSpec as P

EPSILON = 1e-05
NEGATIVE_FLOOR = -1e30
AXIS = "tensor"
F32 = jnp.float32
BF16 = jnp.bfloat16
VMEM = pl.BlockSpec(memory_space=pltpu.VMEM)
SMEM = pl.BlockSpec(memory_space=pltpu.SMEM)
ANY = pl.BlockSpec(memory_space=pl.ANY)
HBM = pl.BlockSpec(memory_space=pltpu.HBM)


def struct(shape, dtype):
    return jax.ShapeDtypeStruct(shape, dtype)


def in_hbm(array):
    return pltpu.with_memory_space_constraint(array, pltpu.HBM)


def params(mebibytes):
    return pltpu.CompilerParams(vmem_limit_bytes=mebibytes << 20)


def scatter_stages(bits):
    if bits < 3:
        return [[bit] for bit in range(bits)]
    return [[0], [1, 2]] + [[bit] for bit in range(3, bits)]


def offsets(group):
    result = [0]
    for bit in reversed(group):
        result = result + [other | (1 << bit) for other in result]
    return result


def positions(stages):
    result = [0]
    for group in stages:
        result = [base | step for base in result for step in offsets(group)]
    return result


def move_bits(value, moves):
    result = value & 0
    for source, target in moves:
        result = result | (((value >> source) & 1) << target)
    return result


def exchange(array, difference, count):
    return lax.ppermute(array, AXIS, [(i, i ^ difference) for i in range(count)])


def project_kernel(
    order, chunks, kv_heads, group, head_size, x_hbm, weight_hbm, first_hbm, count_hbm, keep_ref,
    send_ref, weight, x_ref, first_ref, count_ref, sems, small_sems
):
    rows, steps, depth = x_ref.shape
    width = weight.shape[1]
    chunk = width // chunks
    small = [
        pltpu.make_async_copy(source, target, small_sems.at[i])
        for i, (source, target) in enumerate(
            [(x_hbm, x_ref), (first_hbm, first_ref), (count_hbm, count_ref)]
        )
    ]
    for copy in small:
        copy.start()
    copies = [
        pltpu.make_async_copy(
            weight_hbm.at[:, pl.ds(c * chunk, chunk)], weight.at[:, pl.ds(c * chunk, chunk)], sems.at[c]
        )
        for c in range(chunks)
    ]
    for copy in copies:
        copy.start()
    for copy in small:
        copy.wait()
    slots = len(order)
    half = slots // 2
    me = lax.axis_index(AXIS)
    shape = (steps * slots, rows * steps)
    out_row = lax.broadcasted_iota(jnp.int32, shape, 0)
    place = out_row % slots
    step = out_row // slots
    in_row = lax.broadcasted_iota(jnp.int32, shape, 1)
    bits = range(slots.bit_length() - 1)
    slot = move_bits(place, [(i, order[1 << i].bit_length() - 1) for i in bits]) ^ me
    start = jnp.zeros(shape, jnp.int32)
    length = jnp.zeros(shape, jnp.int32)
    for row in range(rows):
        here = in_row // steps == row
        start = jnp.where(here, first_ref[row], start)
        length = jnp.where(here, count_ref[row], length)
    chosen = (slot >= start) & (slot < start + length) & (in_row % steps == step)
    flat = x_ref[...].reshape(rows * steps, depth)
    picked = jnp.dot(
        jnp.where(chosen, 1.0, 0.0).astype(BF16), flat, preferred_element_type=F32
    ).astype(BF16)
    tile_rows = steps * kv_heads * group
    heads_per_chunk = chunk // head_size
    for c in range(chunks):
        copies[c].wait()
        result = jnp.dot(
            picked, weight[:, c * chunk : (c + 1) * chunk], preferred_element_type=F32
        )
        for local in range(heads_per_chunk):
            head = c * heads_per_chunk + local
            for s in range(steps):
                at = (head // group) * steps * group + s * group + head % group
                block = result[s * slots : (s + 1) * slots, local * head_size : (local + 1) * head_size]
                keep_ref[pl.ds(at, half, stride=tile_rows), :] = block[:half]
                send_ref[pl.ds(at, half, stride=tile_rows), :] = block[half:]


def fetch_kernel(part, cache_hbm, before_ref, cache_ref, after_ref, sems):
    del before_ref, after_ref
    pieces = sems.shape[0]
    span = cache_ref.shape[2] // pieces
    copies = [
        pltpu.make_async_copy(
            cache_hbm.at[:, :, pl.ds((part * pieces + i) * span, span)],
            cache_ref.at[:, :, pl.ds(i * span, span)],
            sems.at[i],
        )
        for i in range(pieces)
    ]
    for copy in copies:
        copy.start()
    for copy in copies:
        copy.wait()


def fetch(cache, part, held):
    return pl.pallas_call(
        functools.partial(fetch_kernel, part),
        out_shape=[
            struct((*cache.shape[:2], cache.shape[2] // 2), cache.dtype),
            struct(held.shape, held.dtype),
        ],
        in_specs=[HBM, ANY],
        out_specs=[VMEM, ANY],
        scratch_shapes=[pltpu.SemaphoreType.DMA((4,))],
        input_output_aliases={1: 1},
        compiler_params=params(1),
        cost_estimate=pl.CostEstimate(flops=0, bytes_accessed=cache.size, transcendentals=0),
    )(in_hbm(cache), held)


def attend_kernel(
    kv_heads, group, steps, query_ref, gain_ref, keys_ref, values_ref, first_ref, count_ref, mask_ref, out_ref
):
    head_size = gain_ref.shape[-1]
    kv_width = kv_heads * head_size
    join = 2 if kv_heads % 2 == 0 else 1
    span = join * head_size
    query = query_ref[...]
    mean = jnp.mean(query * query, axis=1, keepdims=True)
    normed = (query * lax.rsqrt(mean + EPSILON) * gain_ref[...]).astype(BF16)
    me = lax.axis_index(AXIS)
    rows = first_ref.shape[0]

    def find(row, carry):
        owner, tile = carry
        offset = me - first_ref[row]
        inside = (offset >= 0) & (offset < count_ref[row])
        return jnp.where(inside, row, owner), jnp.where(inside, offset, tile)

    owner, tile = lax.fori_loop(0, rows, find, (jnp.int32(0), jnp.int32(0)), unroll=rows <= 16)
    size = steps * group
    row_in_tile = lax.broadcasted_iota(jnp.int32, (size, head_size), 0)
    lane = lax.broadcasted_iota(jnp.int32, (size, head_size), 1)
    stats = jnp.zeros((size, head_size), F32)
    scale = 1.0 / math.sqrt(head_size)
    blank = jnp.zeros((size, head_size), BF16)
    for base in range(0, kv_heads, join):
        at = base * head_size
        keys = keys_ref[0, :, at : at + span]
        left = jnp.concatenate(
            [
                jnp.concatenate(
                    [
                        normed[(base + i) * size : (base + i + 1) * size] if i == j else blank
                        for j in range(join)
                    ],
                    axis=1,
                )
                for i in range(join)
            ],
            axis=0,
        )
        scores = lax.dot_general(
            left, keys, (((1,), (1,)), ((), ())), preferred_element_type=F32
        ) * scale
        top = jnp.max(scores, axis=1, keepdims=True)
        weights = jnp.exp(scores - top).astype(BF16)
        total = jnp.sum(weights.astype(F32), axis=1, keepdims=True)
        values = values_ref[0, :, at : at + span]
        mixed = jnp.dot(weights, values, preferred_element_type=F32) / total
        for i in range(join):
            h = base + i
            rows_here = slice(i * size, (i + 1) * size)
            out_ref[h * size : (h + 1) * size, :] = mixed[
                rows_here, i * head_size : (i + 1) * head_size
            ].astype(BF16)
            here = lane % kv_heads == h
            stats = jnp.where(
                here, jnp.where(lane < 3 * kv_heads, top[rows_here], total[rows_here]), stats
            )
    live = jnp.zeros((size, head_size), jnp.bool_)
    for s in range(steps):
        alive = (tile == 0) | (mask_ref[owner, s, tile] == 1)
        live = live | ((row_in_tile // group == s) & alive)
    stats = jnp.where(live | (lane >= 3 * kv_heads), stats, NEGATIVE_FLOOR)
    high = stats.astype(BF16).astype(F32)
    rest = stats - high
    middle = rest.astype(BF16).astype(F32)
    low = rest - middle
    piece = (lane // kv_heads) % 3
    packed = jnp.where(piece == 0, high, jnp.where(piece == 1, middle, low))
    out_ref[kv_heads * size :, :] = packed.astype(BF16)


def finish_kernel(
    order, kv_heads, group, steps, max_tiles, gate_ref, first_ref, count_ref, tiles_ref, weight_ref, out_ref, stats, turned
):
    rows = first_ref.shape[0]
    head_size = tiles_ref.shape[-1]
    size = steps * group
    block = (kv_heads + 1) * size
    slots = tiles_ref.shape[0]
    me = lax.axis_index(AXIS)
    packed = tiles_ref[:, kv_heads * size :, :].astype(F32).reshape(slots * size, head_size)
    whole = (
        packed
        + pltpu.roll(packed, head_size - kv_heads, 1)
        + pltpu.roll(packed, head_size - 2 * kv_heads, 1)
    )
    stats[0] = whole
    stats[1] = pltpu.roll(whole, head_size - 3 * kv_heads, 1)
    pairs = rows * steps
    moves = [(order[1 << i].bit_length() - 1, i) for i in range(slots.bit_length() - 1)]

    def one_row(row, carry):
        begin = first_ref[row]
        length = count_ref[row]
        places = [
            move_bits(me ^ (begin + jnp.minimum(k, length - 1)), moves) for k in range(max_tiles)
        ]
        tops = []
        for k in range(max_tiles):
            top = stats[0, pl.ds(places[k] * size, size), :]
            tops.append(jnp.where(k < length, top, NEGATIVE_FLOOR))
        best = functools.reduce(jnp.maximum, tops)
        factors = []
        for k in range(max_tiles):
            total = stats[1, pl.ds(places[k] * size, size), :]
            factor = jnp.exp(tops[k] - best) * total
            factors.append(jnp.where(tops[k] > 0.5 * NEGATIVE_FLOOR, factor, 0.0))
        denominator = functools.reduce(jnp.add, factors)
        shares = [factor / denominator for factor in factors]
        for h in range(kv_heads):
            mixed = jnp.zeros((size, head_size), F32)
            for k in range(max_tiles):
                value = tiles_ref[places[k], h * size : (h + 1) * size, :].astype(F32)
                mixed = mixed + shares[k][:, h : h + 1] * value
            for s in range(steps):
                turned[pl.ds(h * group * pairs + row * steps + s, group, stride=pairs), :] = mixed[
                    s * group : (s + 1) * group
                ]
        return carry

    lax.fori_loop(0, rows, one_row, 0)
    total = jnp.zeros((pairs, weight_ref.shape[1]), F32)
    for h in range(kv_heads):
        left = jnp.concatenate(
            [
                turned[(h * group + g) * pairs : (h * group + g + 1) * pairs, :].astype(BF16)
                for g in range(group)
            ],
            axis=1,
        )
        span = group * head_size
        total = total + jnp.dot(
            left, weight_ref[h * span : (h + 1) * span, :], preferred_element_type=F32
        )
    gate = jnp.tanh(jnp.full((1, 1), gate_ref[0], F32))
    result = (total * gate).astype(BF16)
    out_ref[...] = result.reshape(rows, steps, result.shape[1])


def body(
    devices,
    normed_input,
    query_weight,
    query_gain,
    image_cache,
    tile_count,
    image_first_slot,
    cross_tile_mask,
    output_weight,
    output_gate,
):
    rows, steps, depth = normed_input.shape
    head_size = query_gain.shape[0]
    width = query_weight.shape[1]
    heads = width // head_size
    kv_heads = image_cache.shape[2] // (2 * head_size)
    group = heads // kv_heads
    tile_rows = steps * heads
    stages = scatter_stages(devices.bit_length() - 1)
    order = positions(stages)
    half = devices // 2
    chunks = 4
    keep, send = pl.pallas_call(
        functools.partial(project_kernel, order, chunks, kv_heads, group, head_size),
        out_shape=[struct((half * tile_rows, head_size), F32)] * 2,
        in_specs=[HBM] * 4,
        out_specs=[VMEM, VMEM],
        scratch_shapes=[
            pltpu.VMEM((depth, width), BF16),
            pltpu.VMEM(normed_input.shape, BF16),
            pltpu.SMEM(image_first_slot.shape, jnp.int32),
            pltpu.SMEM(tile_count.shape, jnp.int32),
            pltpu.SemaphoreType.DMA((chunks,)),
            pltpu.SemaphoreType.DMA((3,)),
        ],
        compiler_params=params(12),
    )(*[in_hbm(x) for x in (normed_input, query_weight, image_first_slot, tile_count)])
    total = keep + exchange(send, 1, devices)
    cache = []
    for group_bits in stages[1:]:
        steps_out = offsets(group_bits)
        size = total.shape[0] // len(steps_out)
        pieces = [total[i * size : (i + 1) * size] for i in range(len(steps_out))]
        sent = [piece.astype(jnp.float16) for piece in pieces[1:]]
        got = [exchange(piece, step, devices) for piece, step in zip(sent, steps_out[1:])]
        if len(cache) < 2:
            half, pieces[0] = fetch(image_cache, len(cache), pieces[0])
            cache.append(half)
        total = functools.reduce(jnp.add, [pieces[0]] + [piece.astype(F32) for piece in got])
    block = (kv_heads + 1) * steps * group
    tile = pl.pallas_call(
        functools.partial(attend_kernel, kv_heads, group, steps),
        out_shape=struct((block, head_size), BF16),
        in_specs=[VMEM] * 4 + [SMEM] * 3,
        out_specs=VMEM,
        compiler_params=params(6),
    )(total, query_gain, *cache, image_first_slot, tile_count, cross_tile_mask)
    gathered = tile[None]
    for group_bits in reversed(stages):
        gathered = jnp.concatenate(
            [gathered] + [exchange(gathered, step, devices) for step in offsets(group_bits)[1:]], axis=0
        )
    return pl.pallas_call(
        functools.partial(finish_kernel, order, kv_heads, group, steps, cross_tile_mask.shape[2]),
        out_shape=struct((rows, steps, output_weight.shape[1]), BF16),
        in_specs=[SMEM] * 3 + [VMEM, VMEM],
        out_specs=VMEM,
        scratch_shapes=[
            pltpu.VMEM((2, devices * steps * group, head_size), F32),
            pltpu.VMEM((heads * rows * steps, head_size), F32),
        ],
        compiler_params=params(8),
    )(output_gate, image_first_slot, tile_count, gathered, output_weight)


def solution(mesh):
    return jax.shard_map(
        functools.partial(body, mesh.shape[AXIS]),
        mesh=mesh,
        in_specs=(
            P("groups", None, "tensor"),
            P("tensor", None),
            P(),
            P(("groups", "tensor"), None, None),
            P("groups"),
            P("groups"),
            P("groups", None, None),
            P(None, "tensor"),
            P(),
        ),
        out_specs=P("groups", None, "tensor"),
        check_vma=False,
    )
```

```python
import functools
import math

import jax
import jax.numpy as jnp
from jax import lax
from jax.experimental import pallas as pl
from jax.experimental.pallas import tpu as pltpu
from jax.sharding import PartitionSpec as P

EPSILON = 1e-05
NEGATIVE_FLOOR = -1e30
AXIS = "tensor"
F32 = jnp.float32
BF16 = jnp.bfloat16
VMEM = pl.BlockSpec(memory_space=pltpu.VMEM)
SMEM = pl.BlockSpec(memory_space=pltpu.SMEM)
ANY = pl.BlockSpec(memory_space=pl.ANY)
HBM = pl.BlockSpec(memory_space=pltpu.HBM)


def struct(shape, dtype):
    return jax.ShapeDtypeStruct(shape, dtype)


def in_hbm(array):
    return pltpu.with_memory_space_constraint(array, pltpu.HBM)


def params(mebibytes):
    return pltpu.CompilerParams(vmem_limit_bytes=mebibytes << 20)


def exchange_stages(bits):
    if bits < 3:
        return [[1 << bit] for bit in range(bits)]
    return [[1], [4, 3]] + [[(1 << bit) | 1] for bit in range(3, bits)]


def offsets(group):
    result = [0]
    for difference in group:
        result = result + [other ^ difference for other in result]
    return result


def positions(stages):
    result = [0]
    for group in stages:
        result = [base ^ step for base in result for step in offsets(group)]
    return result


def combine_bits(value, masks):
    result = value & 0
    for bit, mask in enumerate(masks):
        result = result ^ (((value >> bit) & 1) * mask)
    return result


def exchange(array, difference, count):
    return lax.ppermute(array, AXIS, [(i, i ^ difference) for i in range(count)])


def project_kernel(
    order, chunks, kv_heads, group, head_size, x_hbm, weight_hbm, first_hbm, count_hbm, keep_ref,
    send_ref, weight, x_ref, first_ref, count_ref, sems, small_sems
):
    rows, steps, depth = x_ref.shape
    width = weight.shape[1]
    chunk = width // chunks
    small = [
        pltpu.make_async_copy(source, target, small_sems.at[i])
        for i, (source, target) in enumerate(
            [(x_hbm, x_ref), (first_hbm, first_ref), (count_hbm, count_ref)]
        )
    ]
    for copy in small:
        copy.start()
    copies = [
        pltpu.make_async_copy(
            weight_hbm.at[:, pl.ds(c * chunk, chunk)], weight.at[:, pl.ds(c * chunk, chunk)], sems.at[c]
        )
        for c in range(chunks)
    ]
    for copy in copies:
        copy.start()
    for copy in small:
        copy.wait()
    slots = len(order)
    half = slots // 2
    me = lax.axis_index(AXIS)
    shape = (steps * slots, rows * steps)
    out_row = lax.broadcasted_iota(jnp.int32, shape, 0)
    place = out_row % slots
    step = out_row // slots
    in_row = lax.broadcasted_iota(jnp.int32, shape, 1)
    slot = combine_bits(place, [order[1 << i] for i in range(slots.bit_length() - 1)]) ^ me
    start = jnp.zeros(shape, jnp.int32)
    length = jnp.zeros(shape, jnp.int32)
    for row in range(rows):
        here = in_row // steps == row
        start = jnp.where(here, first_ref[row], start)
        length = jnp.where(here, count_ref[row], length)
    chosen = (slot >= start) & (slot < start + length) & (in_row % steps == step)
    flat = x_ref[...].reshape(rows * steps, depth)
    picked = jnp.dot(
        jnp.where(chosen, 1.0, 0.0).astype(BF16), flat, preferred_element_type=F32
    ).astype(BF16)
    tile_rows = steps * kv_heads * group
    heads_per_chunk = chunk // head_size
    for c in range(chunks):
        copies[c].wait()
        result = jnp.dot(
            picked, weight[:, c * chunk : (c + 1) * chunk], preferred_element_type=F32
        )
        for local in range(heads_per_chunk):
            head = c * heads_per_chunk + local
            for s in range(steps):
                at = (head // group) * steps * group + s * group + head % group
                block = result[s * slots : (s + 1) * slots, local * head_size : (local + 1) * head_size]
                keep_ref[pl.ds(at, half, stride=tile_rows), :] = block[:half]
                send_ref[pl.ds(at, half, stride=tile_rows), :] = block[half:]


def fetch_kernel(part, cache_hbm, before_ref, gate_ref, cache_ref, after_ref, tanh_ref, sems):
    del before_ref, after_ref
    pieces = sems.shape[0]
    span = cache_ref.shape[2] // pieces
    copies = [
        pltpu.make_async_copy(
            cache_hbm.at[:, :, pl.ds((part * pieces + i) * span, span)],
            cache_ref.at[:, :, pl.ds(i * span, span)],
            sems.at[i],
        )
        for i in range(pieces)
    ]
    for copy in copies:
        copy.start()
    tanh_ref[...] = jnp.tanh(jnp.full(tanh_ref.shape, gate_ref[0], F32))
    for copy in copies:
        copy.wait()


def fetch(cache, part, held, gate):
    return pl.pallas_call(
        functools.partial(fetch_kernel, part),
        out_shape=[
            struct((*cache.shape[:2], cache.shape[2] // 2), cache.dtype),
            struct(held.shape, held.dtype),
            struct((8, 128), F32),
        ],
        in_specs=[HBM, ANY, SMEM],
        out_specs=[VMEM, ANY, VMEM],
        scratch_shapes=[pltpu.SemaphoreType.DMA((4,))],
        input_output_aliases={1: 1},
        compiler_params=params(1),
        cost_estimate=pl.CostEstimate(flops=0, bytes_accessed=cache.size, transcendentals=0),
    )(in_hbm(cache), held, gate)


def attend_kernel(
    kv_heads, group, steps, query_ref, gain_ref, keys_ref, values_ref, first_ref, count_ref, mask_ref, out_ref
):
    head_size = gain_ref.shape[-1]
    kv_width = kv_heads * head_size
    join = 2 if kv_heads % 2 == 0 else 1
    span = join * head_size
    query = query_ref[...]
    mean = jnp.mean(query * query, axis=1, keepdims=True)
    normed = (query * lax.rsqrt(mean + EPSILON) * gain_ref[...]).astype(BF16)
    me = lax.axis_index(AXIS)
    rows = first_ref.shape[0]

    def find(row, carry):
        owner, tile = carry
        offset = me - first_ref[row]
        inside = (offset >= 0) & (offset < count_ref[row])
        return jnp.where(inside, row, owner), jnp.where(inside, offset, tile)

    owner, tile = lax.fori_loop(0, rows, find, (jnp.int32(0), jnp.int32(0)), unroll=rows <= 16)
    size = steps * group
    row_in_tile = lax.broadcasted_iota(jnp.int32, (size, head_size), 0)
    lane = lax.broadcasted_iota(jnp.int32, (size, head_size), 1)
    stats = jnp.zeros((size, head_size), F32)
    scale = 1.0 / math.sqrt(head_size)
    blank = jnp.zeros((size, head_size), BF16)
    bases = range(0, kv_heads, join)
    scores = []
    for base in bases:
        keys = keys_ref[0, :, base * head_size : (base + join) * head_size]
        left = jnp.concatenate(
            [
                jnp.concatenate(
                    [
                        normed[(base + i) * size : (base + i + 1) * size] if i == j else blank
                        for j in range(join)
                    ],
                    axis=1,
                )
                for i in range(join)
            ],
            axis=0,
        )
        scores.append(
            lax.dot_general(left, keys, (((1,), (1,)), ((), ())), preferred_element_type=F32) * scale
        )
    tops = [jnp.max(score, axis=1, keepdims=True) for score in scores]
    weights = [jnp.exp(score - top).astype(BF16) for score, top in zip(scores, tops)]
    totals = [jnp.sum(weight.astype(F32), axis=1, keepdims=True) for weight in weights]
    for base, top, weight, total in zip(bases, tops, weights, totals):
        values = values_ref[0, :, base * head_size : (base + join) * head_size]
        mixed = jnp.dot(weight, values, preferred_element_type=F32) / total
        for i in range(join):
            h = base + i
            rows_here = slice(i * size, (i + 1) * size)
            out_ref[h * size : (h + 1) * size, :] = mixed[
                rows_here, i * head_size : (i + 1) * head_size
            ].astype(BF16)
            here = lane % kv_heads == h
            stats = jnp.where(
                here, jnp.where(lane < 3 * kv_heads, top[rows_here], total[rows_here]), stats
            )
    live = jnp.zeros((size, head_size), jnp.bool_)
    for s in range(steps):
        alive = (tile == 0) | (mask_ref[owner, s, tile] == 1)
        live = live | ((row_in_tile // group == s) & alive)
    stats = jnp.where(live | (lane >= 3 * kv_heads), stats, NEGATIVE_FLOOR)
    high = stats.astype(BF16).astype(F32)
    rest = stats - high
    middle = rest.astype(BF16).astype(F32)
    low = rest - middle
    piece = (lane // kv_heads) % 3
    packed = jnp.where(piece == 0, high, jnp.where(piece == 1, middle, low))
    out_ref[kv_heads * size :, :] = packed.astype(BF16)


def finish_kernel(
    order, kv_heads, group, steps, max_tiles, gate_ref, first_ref, count_ref, tiles_ref, weight_ref,
    out_ref, stats, turned
):
    rows = first_ref.shape[0]
    head_size = tiles_ref.shape[-1]
    size = steps * group
    block = (kv_heads + 1) * size
    slots = tiles_ref.shape[0]
    me = lax.axis_index(AXIS)
    packed = tiles_ref[:, kv_heads * size :, :].astype(F32).reshape(slots * size, head_size)
    whole = (
        packed
        + pltpu.roll(packed, head_size - kv_heads, 1)
        + pltpu.roll(packed, head_size - 2 * kv_heads, 1)
    )
    stats[0] = whole
    stats[1] = pltpu.roll(whole, head_size - 3 * kv_heads, 1)
    pairs = rows * steps
    masks = [order.index(1 << i) for i in range(slots.bit_length() - 1)]

    def one_row(row, carry):
        begin = first_ref[row]
        length = count_ref[row]
        places = [
            combine_bits(me ^ (begin + jnp.minimum(k, length - 1)), masks) for k in range(max_tiles)
        ]
        tops = []
        for k in range(max_tiles):
            top = stats[0, pl.ds(places[k] * size, size), :]
            tops.append(jnp.where(k < length, top, NEGATIVE_FLOOR))
        best = functools.reduce(jnp.maximum, tops)
        factors = []
        for k in range(max_tiles):
            total = stats[1, pl.ds(places[k] * size, size), :]
            factor = jnp.exp(tops[k] - best) * total
            factors.append(jnp.where(tops[k] > 0.5 * NEGATIVE_FLOOR, factor, 0.0))
        denominator = functools.reduce(jnp.add, factors)
        shares = [factor / denominator for factor in factors]
        for h in range(kv_heads):
            mixed = jnp.zeros((size, head_size), F32)
            for k in range(max_tiles):
                value = tiles_ref[places[k], h * size : (h + 1) * size, :].astype(F32)
                mixed = mixed + shares[k][:, h : h + 1] * value
            for s in range(steps):
                turned[pl.ds(h * group * pairs + row * steps + s, group, stride=pairs), :] = mixed[
                    s * group : (s + 1) * group
                ]
        return carry

    lax.fori_loop(0, rows, one_row, 0, unroll=8)
    total = jnp.zeros((pairs, weight_ref.shape[1]), F32)
    for h in range(kv_heads):
        left = jnp.concatenate(
            [
                turned[(h * group + g) * pairs : (h * group + g + 1) * pairs, :].astype(BF16)
                for g in range(group)
            ],
            axis=1,
        )
        span = group * head_size
        total = total + jnp.dot(
            left, weight_ref[h * span : (h + 1) * span, :], preferred_element_type=F32
        )
    gate = gate_ref[:1, :1]
    result = (total * gate).astype(BF16)
    out_ref[...] = result.reshape(rows, steps, result.shape[1])


def body(
    devices,
    normed_input,
    query_weight,
    query_gain,
    image_cache,
    tile_count,
    image_first_slot,
    cross_tile_mask,
    output_weight,
    output_gate,
):
    rows, steps, depth = normed_input.shape
    head_size = query_gain.shape[0]
    width = query_weight.shape[1]
    heads = width // head_size
    kv_heads = image_cache.shape[2] // (2 * head_size)
    group = heads // kv_heads
    tile_rows = steps * heads
    stages = exchange_stages(devices.bit_length() - 1)
    order = positions(stages)
    half = devices // 2
    chunks = 4
    keep, send = pl.pallas_call(
        functools.partial(project_kernel, order, chunks, kv_heads, group, head_size),
        out_shape=[struct((half * tile_rows, head_size), F32)] * 2,
        in_specs=[HBM] * 4,
        out_specs=[VMEM, VMEM],
        scratch_shapes=[
            pltpu.VMEM((depth, width), BF16),
            pltpu.VMEM(normed_input.shape, BF16),
            pltpu.SMEM(image_first_slot.shape, jnp.int32),
            pltpu.SMEM(tile_count.shape, jnp.int32),
            pltpu.SemaphoreType.DMA((chunks,)),
            pltpu.SemaphoreType.DMA((3,)),
        ],
        compiler_params=params(12),
    )(*[in_hbm(x) for x in (normed_input, query_weight, image_first_slot, tile_count)])
    total = keep + exchange(send, 1, devices)
    cache = []
    for group_bits in stages[1:]:
        steps_out = offsets(group_bits)
        size = total.shape[0] // len(steps_out)
        pieces = [total[i * size : (i + 1) * size] for i in range(len(steps_out))]
        sent = [piece.astype(jnp.float16) for piece in pieces[1:]]
        got = [exchange(piece, step, devices) for piece, step in zip(sent, steps_out[1:])]
        if len(cache) < 2:
            half, pieces[0], gate = fetch(image_cache, len(cache), pieces[0], output_gate)
            cache.append(half)
        total = functools.reduce(jnp.add, [pieces[0]] + [piece.astype(F32) for piece in got])
    block = (kv_heads + 1) * steps * group
    tile = pl.pallas_call(
        functools.partial(attend_kernel, kv_heads, group, steps),
        out_shape=struct((block, head_size), BF16),
        in_specs=[VMEM] * 4 + [SMEM] * 3,
        out_specs=VMEM,
        compiler_params=params(6),
    )(total, query_gain, *cache, image_first_slot, tile_count, cross_tile_mask)
    gathered = tile[None]
    for group_bits in reversed(stages):
        gathered = jnp.concatenate(
            [gathered] + [exchange(gathered, step, devices) for step in offsets(group_bits)[1:]], axis=0
        )
    return pl.pallas_call(
        functools.partial(finish_kernel, order, kv_heads, group, steps, cross_tile_mask.shape[2]),
        out_shape=struct((rows, steps, output_weight.shape[1]), BF16),
        in_specs=[VMEM, SMEM, SMEM, VMEM, VMEM],
        out_specs=VMEM,
        scratch_shapes=[
            pltpu.VMEM((2, devices * steps * group, head_size), F32),
            pltpu.VMEM((heads * rows * steps, head_size), F32),
        ],
        compiler_params=params(8),
    )(gate, image_first_slot, tile_count, gathered, output_weight)


def solution(mesh):
    return jax.shard_map(
        functools.partial(body, mesh.shape[AXIS]),
        mesh=mesh,
        in_specs=(
            P("groups", None, "tensor"),
            P("tensor", None),
            P(),
            P(("groups", "tensor"), None, None),
            P("groups"),
            P("groups"),
            P("groups", None, None),
            P(None, "tensor"),
            P(),
        ),
        out_specs=P("groups", None, "tensor"),
        check_vma=False,
    )
```

```python
import functools
import math

import jax
import jax.numpy as jnp
from jax import lax
from jax.experimental import pallas as pl
from jax.experimental.pallas import tpu as pltpu
from jax.sharding import PartitionSpec as P

EPSILON = 1e-05
NEGATIVE_FLOOR = -1e30
AXIS = "tensor"
F32 = jnp.float32
BF16 = jnp.bfloat16
VMEM = pl.BlockSpec(memory_space=pltpu.VMEM)
SMEM = pl.BlockSpec(memory_space=pltpu.SMEM)
ANY = pl.BlockSpec(memory_space=pl.ANY)
HBM = pl.BlockSpec(memory_space=pltpu.HBM)


def struct(shape, dtype):
    return jax.ShapeDtypeStruct(shape, dtype)


def in_hbm(array):
    return pltpu.with_memory_space_constraint(array, pltpu.HBM)


def params(mebibytes):
    return pltpu.CompilerParams(vmem_limit_bytes=mebibytes << 20)


def exchange_stages(bits):
    if bits < 3:
        return [[1 << bit] for bit in range(bits)]
    return [[1], [4, 3]] + [[(1 << bit) | 1] for bit in range(3, bits)]


def offsets(group):
    result = [0]
    for difference in group:
        result = result + [other ^ difference for other in result]
    return result


def positions(stages):
    result = [0]
    for group in stages:
        result = [base ^ step for base in result for step in offsets(group)]
    return result


def combine_bits(value, masks):
    result = value & 0
    for bit, mask in enumerate(masks):
        result = result ^ (((value >> bit) & 1) * mask)
    return result


def exchange(array, difference, count):
    return lax.ppermute(array, AXIS, [(i, i ^ difference) for i in range(count)])


def project_kernel(
    order, chunks, kv_heads, group, head_size, x_hbm, weight_hbm, first_hbm, count_hbm, keep_ref,
    send_ref, weight, x_ref, first_ref, count_ref, sems, small_sems
):
    rows, steps, depth = x_ref.shape
    width = weight.shape[1]
    chunk = width // chunks
    small = [
        pltpu.make_async_copy(source, target, small_sems.at[i])
        for i, (source, target) in enumerate(
            [(x_hbm, x_ref), (first_hbm, first_ref), (count_hbm, count_ref)]
        )
    ]
    for copy in small:
        copy.start()
    copies = [
        pltpu.make_async_copy(
            weight_hbm.at[:, pl.ds(c * chunk, chunk)], weight.at[:, pl.ds(c * chunk, chunk)], sems.at[c]
        )
        for c in range(chunks)
    ]
    for copy in copies:
        copy.start()
    for copy in small:
        copy.wait()
    slots = len(order)
    half = slots // 2
    me = lax.axis_index(AXIS)
    shape = (steps * slots, rows * steps)
    out_row = lax.broadcasted_iota(jnp.int32, shape, 0)
    place = out_row % slots
    step = out_row // slots
    in_row = lax.broadcasted_iota(jnp.int32, shape, 1)
    slot = combine_bits(place, [order[1 << i] for i in range(slots.bit_length() - 1)]) ^ me
    start = jnp.zeros(shape, jnp.int32)
    length = jnp.zeros(shape, jnp.int32)
    for row in range(rows):
        here = in_row // steps == row
        start = jnp.where(here, first_ref[row], start)
        length = jnp.where(here, count_ref[row], length)
    chosen = (slot >= start) & (slot < start + length) & (in_row % steps == step)
    flat = x_ref[...].reshape(rows * steps, depth)
    picked = jnp.dot(
        jnp.where(chosen, 1.0, 0.0).astype(BF16), flat, preferred_element_type=F32
    ).astype(BF16)
    tile_rows = steps * kv_heads * group
    heads_per_chunk = chunk // head_size
    for c in range(chunks):
        copies[c].wait()
        result = jnp.dot(
            picked, weight[:, c * chunk : (c + 1) * chunk], preferred_element_type=F32
        )
        for local in range(heads_per_chunk):
            head = c * heads_per_chunk + local
            for s in range(steps):
                at = (head // group) * steps * group + s * group + head % group
                block = result[s * slots : (s + 1) * slots, local * head_size : (local + 1) * head_size]
                keep_ref[pl.ds(at, half, stride=tile_rows), :] = block[:half]
                send_ref[pl.ds(at, half, stride=tile_rows), :] = block[half:]


def fetch_kernel(part, cache_hbm, before_ref, gate_ref, cache_ref, after_ref, tanh_ref, sems):
    del before_ref, after_ref
    pieces = sems.shape[0]
    span = cache_ref.shape[2] // pieces
    copies = [
        pltpu.make_async_copy(
            cache_hbm.at[:, :, pl.ds((part * pieces + i) * span, span)],
            cache_ref.at[:, :, pl.ds(i * span, span)],
            sems.at[i],
        )
        for i in range(pieces)
    ]
    for copy in copies:
        copy.start()
    tanh_ref[...] = jnp.tanh(jnp.full(tanh_ref.shape, gate_ref[0], F32))
    for copy in copies:
        copy.wait()


def fetch(cache, part, held, gate):
    return pl.pallas_call(
        functools.partial(fetch_kernel, part),
        out_shape=[
            struct((*cache.shape[:2], cache.shape[2] // 2), cache.dtype),
            struct(held.shape, held.dtype),
            struct((8, 128), F32),
        ],
        in_specs=[HBM, ANY, SMEM],
        out_specs=[VMEM, ANY, VMEM],
        scratch_shapes=[pltpu.SemaphoreType.DMA((4,))],
        input_output_aliases={1: 1},
        compiler_params=params(1),
        cost_estimate=pl.CostEstimate(flops=0, bytes_accessed=cache.size, transcendentals=0),
    )(in_hbm(cache), held, gate)


def attend_kernel(
    kv_heads, group, steps, query_ref, gain_ref, keys_ref, values_ref, first_in, count_in, mask_in,
    out_ref, first_ref, count_ref, mask_ref, sems
):
    copies = [
        pltpu.make_async_copy(first_in, first_ref, sems.at[0]),
        pltpu.make_async_copy(count_in, count_ref, sems.at[1]),
        pltpu.make_async_copy(mask_in, mask_ref, sems.at[2]),
    ]
    for copy in copies:
        copy.start()
    head_size = gain_ref.shape[-1]
    kv_width = kv_heads * head_size
    join = 2 if kv_heads % 2 == 0 else 1
    span = join * head_size
    query = query_ref[...]
    mean = jnp.mean(query * query, axis=1, keepdims=True)
    normed = (query * lax.rsqrt(mean + EPSILON) * gain_ref[...]).astype(BF16)
    me = lax.axis_index(AXIS)
    size = steps * group
    row_in_tile = lax.broadcasted_iota(jnp.int32, (size, head_size), 0)
    lane = lax.broadcasted_iota(jnp.int32, (size, head_size), 1)
    stats = jnp.zeros((size, head_size), F32)
    scale = 1.0 / math.sqrt(head_size)
    blank = jnp.zeros((size, head_size), BF16)
    bases = range(0, kv_heads, join)
    scores = []
    for base in bases:
        keys = keys_ref[0, :, base * head_size : (base + join) * head_size]
        left = jnp.concatenate(
            [
                jnp.concatenate(
                    [
                        normed[(base + i) * size : (base + i + 1) * size] if i == j else blank
                        for j in range(join)
                    ],
                    axis=1,
                )
                for i in range(join)
            ],
            axis=0,
        )
        scores.append(
            lax.dot_general(left, keys, (((1,), (1,)), ((), ())), preferred_element_type=F32) * scale
        )
    tops = [jnp.max(score, axis=1, keepdims=True) for score in scores]
    weights = [jnp.exp(score - top).astype(BF16) for score, top in zip(scores, tops)]
    totals = [jnp.sum(weight.astype(F32), axis=1, keepdims=True) for weight in weights]
    for base, top, weight, total in zip(bases, tops, weights, totals):
        values = values_ref[0, :, base * head_size : (base + join) * head_size]
        mixed = jnp.dot(weight, values, preferred_element_type=F32) / total
        for i in range(join):
            h = base + i
            rows_here = slice(i * size, (i + 1) * size)
            out_ref[h * size : (h + 1) * size, :] = mixed[
                rows_here, i * head_size : (i + 1) * head_size
            ].astype(BF16)
            here = lane % kv_heads == h
            stats = jnp.where(
                here, jnp.where(lane < 3 * kv_heads, top[rows_here], total[rows_here]), stats
            )
    for copy in copies:
        copy.wait()
    rows = first_ref.shape[0]

    def find(row, carry):
        owner, tile = carry
        offset = me - first_ref[row]
        inside = (offset >= 0) & (offset < count_ref[row])
        return jnp.where(inside, row, owner), jnp.where(inside, offset, tile)

    owner, tile = lax.fori_loop(0, rows, find, (jnp.int32(0), jnp.int32(0)), unroll=rows <= 16)
    live = jnp.zeros((size, head_size), jnp.bool_)
    for s in range(steps):
        alive = (tile == 0) | (mask_ref[owner, s, tile] == 1)
        live = live | ((row_in_tile // group == s) & alive)
    stats = jnp.where(live | (lane >= 3 * kv_heads), stats, NEGATIVE_FLOOR)
    high = stats.astype(BF16).astype(F32)
    rest = stats - high
    middle = rest.astype(BF16).astype(F32)
    low = rest - middle
    piece = (lane // kv_heads) % 3
    packed = jnp.where(piece == 0, high, jnp.where(piece == 1, middle, low))
    out_ref[kv_heads * size :, :] = packed.astype(BF16)


def finish_kernel(
    order, kv_heads, group, steps, max_tiles, gate_ref, first_ref, count_ref, tiles_ref, weight_ref,
    out_ref, stats, turned
):
    rows = first_ref.shape[0]
    head_size = tiles_ref.shape[-1]
    size = steps * group
    block = (kv_heads + 1) * size
    slots = tiles_ref.shape[0]
    me = lax.axis_index(AXIS)
    packed = tiles_ref[:, kv_heads * size :, :].astype(F32).reshape(slots * size, head_size)
    whole = (
        packed
        + pltpu.roll(packed, head_size - kv_heads, 1)
        + pltpu.roll(packed, head_size - 2 * kv_heads, 1)
    )
    stats[0] = whole
    stats[1] = pltpu.roll(whole, head_size - 3 * kv_heads, 1)
    first = first_ref[...].reshape(1, rows)
    count = count_ref[...].reshape(1, rows)
    pairs = rows * steps
    masks = [order.index(1 << i) for i in range(slots.bit_length() - 1)]

    def one_row(row, carry):
        here = (lax.broadcasted_iota(jnp.int32, (1, rows), 1) == row).astype(jnp.int32)
        begin = jnp.sum(first * here)
        length = jnp.sum(count * here)
        places = [
            combine_bits(me ^ (begin + jnp.minimum(k, length - 1)), masks) for k in range(max_tiles)
        ]
        tops = []
        for k in range(max_tiles):
            top = stats[0, pl.ds(places[k] * size, size), :]
            tops.append(jnp.where(k < length, top, NEGATIVE_FLOOR))
        best = functools.reduce(jnp.maximum, tops)
        factors = []
        for k in range(max_tiles):
            total = stats[1, pl.ds(places[k] * size, size), :]
            factor = jnp.exp(tops[k] - best) * total
            factors.append(jnp.where(tops[k] > 0.5 * NEGATIVE_FLOOR, factor, 0.0))
        denominator = functools.reduce(jnp.add, factors)
        shares = [factor / denominator for factor in factors]
        for h in range(kv_heads):
            mixed = jnp.zeros((size, head_size), F32)
            for k in range(max_tiles):
                value = tiles_ref[places[k], h * size : (h + 1) * size, :].astype(F32)
                mixed = mixed + shares[k][:, h : h + 1] * value
            for s in range(steps):
                turned[pl.ds(h * group * pairs + row * steps + s, group, stride=pairs), :] = mixed[
                    s * group : (s + 1) * group
                ]
        return carry

    lax.fori_loop(0, rows, one_row, 0, unroll=8)
    total = jnp.zeros((pairs, weight_ref.shape[1]), F32)
    for h in range(kv_heads):
        left = jnp.concatenate(
            [
                turned[(h * group + g) * pairs : (h * group + g + 1) * pairs, :].astype(BF16)
                for g in range(group)
            ],
            axis=1,
        )
        span = group * head_size
        total = total + jnp.dot(
            left, weight_ref[h * span : (h + 1) * span, :], preferred_element_type=F32
        )
    gate = gate_ref[:1, :1]
    result = (total * gate).astype(BF16)
    out_ref[...] = result.reshape(rows, steps, result.shape[1])


def body(
    devices,
    normed_input,
    query_weight,
    query_gain,
    image_cache,
    tile_count,
    image_first_slot,
    cross_tile_mask,
    output_weight,
    output_gate,
):
    rows, steps, depth = normed_input.shape
    head_size = query_gain.shape[0]
    width = query_weight.shape[1]
    heads = width // head_size
    kv_heads = image_cache.shape[2] // (2 * head_size)
    group = heads // kv_heads
    tile_rows = steps * heads
    stages = exchange_stages(devices.bit_length() - 1)
    order = positions(stages)
    half = devices // 2
    chunks = 4
    keep, send = pl.pallas_call(
        functools.partial(project_kernel, order, chunks, kv_heads, group, head_size),
        out_shape=[struct((half * tile_rows, head_size), F32)] * 2,
        in_specs=[HBM] * 4,
        out_specs=[VMEM, VMEM],
        scratch_shapes=[
            pltpu.VMEM((depth, width), BF16),
            pltpu.VMEM(normed_input.shape, BF16),
            pltpu.SMEM(image_first_slot.shape, jnp.int32),
            pltpu.SMEM(tile_count.shape, jnp.int32),
            pltpu.SemaphoreType.DMA((chunks,)),
            pltpu.SemaphoreType.DMA((3,)),
        ],
        compiler_params=params(12),
    )(*[in_hbm(x) for x in (normed_input, query_weight, image_first_slot, tile_count)])
    total = keep + exchange(send, 1, devices)
    cache = []
    for group_bits in stages[1:]:
        steps_out = offsets(group_bits)
        size = total.shape[0] // len(steps_out)
        pieces = [total[i * size : (i + 1) * size] for i in range(len(steps_out))]
        sent = [piece.astype(jnp.float16) for piece in pieces[1:]]
        got = [exchange(piece, step, devices) for piece, step in zip(sent, steps_out[1:])]
        if len(cache) < 2:
            half, pieces[0], gate = fetch(image_cache, len(cache), pieces[0], output_gate)
            cache.append(half)
        total = functools.reduce(jnp.add, [pieces[0]] + [piece.astype(F32) for piece in got])
    block = (kv_heads + 1) * steps * group
    tile = pl.pallas_call(
        functools.partial(attend_kernel, kv_heads, group, steps),
        out_shape=struct((block, head_size), BF16),
        in_specs=[VMEM] * 7,
        out_specs=VMEM,
        scratch_shapes=[
            pltpu.SMEM(image_first_slot.shape, jnp.int32),
            pltpu.SMEM(tile_count.shape, jnp.int32),
            pltpu.SMEM(cross_tile_mask.shape, jnp.int32),
            pltpu.SemaphoreType.DMA((3,)),
        ],
        compiler_params=params(6),
    )(total, query_gain, *cache, image_first_slot, tile_count, cross_tile_mask)
    gathered = tile[None]
    for group_bits in reversed(stages):
        gathered = jnp.concatenate(
            [gathered] + [exchange(gathered, step, devices) for step in offsets(group_bits)[1:]], axis=0
        )
    scratch = 4 * head_size * (2 * devices * steps * group + heads * rows * steps)
    return pl.pallas_call(
        functools.partial(finish_kernel, order, kv_heads, group, steps, cross_tile_mask.shape[2]),
        out_shape=struct((rows, steps, output_weight.shape[1]), BF16),
        in_specs=[VMEM] * 5,
        out_specs=VMEM,
        scratch_shapes=[
            pltpu.VMEM((2, devices * steps * group, head_size), F32),
            pltpu.VMEM((heads * rows * steps, head_size), F32),
        ],
        compiler_params=params(6 + (2 * scratch >> 20)),
    )(gate, image_first_slot, tile_count, gathered, output_weight)


def solution(mesh):
    return jax.shard_map(
        functools.partial(body, mesh.shape[AXIS]),
        mesh=mesh,
        in_specs=(
            P("groups", None, "tensor"),
            P("tensor", None),
            P(),
            P(("groups", "tensor"), None, None),
            P("groups"),
            P("groups"),
            P("groups", None, None),
            P(None, "tensor"),
            P(),
        ),
        out_specs=P("groups", None, "tensor"),
        check_vma=False,
    )
```

```python
import functools
import math

import jax
import jax.numpy as jnp
from jax import lax
from jax.experimental import pallas as pl
from jax.experimental.pallas import tpu as pltpu
from jax.sharding import PartitionSpec as P

EPSILON = 1e-05
NEGATIVE_FLOOR = -1e30
AXIS = "tensor"
F32 = jnp.float32
BF16 = jnp.bfloat16
VMEM = pl.BlockSpec(memory_space=pltpu.VMEM)
SMEM = pl.BlockSpec(memory_space=pltpu.SMEM)
ANY = pl.BlockSpec(memory_space=pl.ANY)
HBM = pl.BlockSpec(memory_space=pltpu.HBM)


def struct(shape, dtype):
    return jax.ShapeDtypeStruct(shape, dtype)


def in_hbm(array):
    return pltpu.with_memory_space_constraint(array, pltpu.HBM)


def params(mebibytes):
    return pltpu.CompilerParams(vmem_limit_bytes=mebibytes << 20)


def exchange_stages(bits):
    if bits < 3:
        return [[1 << bit] for bit in range(bits)]
    return [[1], [4, 3]] + [[(1 << bit) | 1] for bit in range(3, bits)]


def offsets(group):
    result = [0]
    for difference in group:
        result = result + [other ^ difference for other in result]
    return result


def positions(stages):
    result = [0]
    for group in stages:
        result = [base ^ step for base in result for step in offsets(group)]
    return result


def combine_bits(value, masks):
    result = value & 0
    for bit, mask in enumerate(masks):
        result = result ^ (((value >> bit) & 1) * mask)
    return result


def exchange(array, difference, count):
    return lax.ppermute(array, AXIS, [(i, i ^ difference) for i in range(count)])


def project_kernel(
    order, chunks, kv_heads, group, head_size, x_hbm, weight_hbm, first_hbm, count_hbm, keep_ref,
    send_ref, weight, x_ref, first_ref, count_ref, sems, small_sems
):
    rows, steps, depth = x_ref.shape
    width = weight.shape[1]
    chunk = width // chunks
    small = [
        pltpu.make_async_copy(source, target, small_sems.at[i])
        for i, (source, target) in enumerate(
            [(x_hbm, x_ref), (first_hbm, first_ref), (count_hbm, count_ref)]
        )
    ]
    for copy in small:
        copy.start()
    copies = [
        pltpu.make_async_copy(
            weight_hbm.at[:, pl.ds(c * chunk, chunk)], weight.at[:, pl.ds(c * chunk, chunk)], sems.at[c]
        )
        for c in range(chunks)
    ]
    for copy in copies:
        copy.start()
    for copy in small:
        copy.wait()
    slots = len(order)
    half = slots // 2
    me = lax.axis_index(AXIS)
    shape = (steps * slots, rows * steps)
    out_row = lax.broadcasted_iota(jnp.int32, shape, 0)
    place = out_row % slots
    step = out_row // slots
    in_row = lax.broadcasted_iota(jnp.int32, shape, 1)
    slot = combine_bits(place, [order[1 << i] for i in range(slots.bit_length() - 1)]) ^ me
    start = jnp.zeros(shape, jnp.int32)
    length = jnp.zeros(shape, jnp.int32)
    for row in range(rows):
        here = in_row // steps == row
        start = jnp.where(here, first_ref[row], start)
        length = jnp.where(here, count_ref[row], length)
    chosen = (slot >= start) & (slot < start + length) & (in_row % steps == step)
    flat = x_ref[...].reshape(rows * steps, depth)
    picked = jnp.dot(
        jnp.where(chosen, 1.0, 0.0).astype(BF16), flat, preferred_element_type=F32
    ).astype(BF16)
    tile_rows = steps * kv_heads * group
    heads_per_chunk = chunk // head_size
    for c in range(chunks):
        copies[c].wait()
        result = jnp.dot(
            picked, weight[:, c * chunk : (c + 1) * chunk], preferred_element_type=F32
        )
        for local in range(heads_per_chunk):
            head = c * heads_per_chunk + local
            for s in range(steps):
                at = (head // group) * steps * group + s * group + head % group
                block = result[s * slots : (s + 1) * slots, local * head_size : (local + 1) * head_size]
                keep_ref[pl.ds(at, half, stride=tile_rows), :] = block[:half]
                send_ref[pl.ds(at, half, stride=tile_rows), :] = block[half:]


def fetch_kernel(part, cache_hbm, before_ref, gate_ref, cache_ref, after_ref, tanh_ref, sems):
    del before_ref, after_ref
    pieces = sems.shape[0]
    span = cache_ref.shape[2] // pieces
    copies = [
        pltpu.make_async_copy(
            cache_hbm.at[:, :, pl.ds((part * pieces + i) * span, span)],
            cache_ref.at[:, :, pl.ds(i * span, span)],
            sems.at[i],
        )
        for i in range(pieces)
    ]
    for copy in copies:
        copy.start()
    tanh_ref[...] = jnp.tanh(jnp.full(tanh_ref.shape, gate_ref[0], F32))
    for copy in copies:
        copy.wait()


def fetch(cache, part, held, gate):
    return pl.pallas_call(
        functools.partial(fetch_kernel, part),
        out_shape=[
            struct((*cache.shape[:2], cache.shape[2] // 2), cache.dtype),
            struct(held.shape, held.dtype),
            struct((8, 128), F32),
        ],
        in_specs=[HBM, ANY, SMEM],
        out_specs=[VMEM, ANY, VMEM],
        scratch_shapes=[pltpu.SemaphoreType.DMA((4,))],
        input_output_aliases={1: 1},
        compiler_params=params(1),
        cost_estimate=pl.CostEstimate(flops=0, bytes_accessed=cache.size, transcendentals=0),
    )(in_hbm(cache), held, gate)


def attend_kernel(
    kv_heads, group, steps, query_ref, gain_ref, keys_ref, values_ref, first_in, count_in, mask_in,
    out_ref, first_ref, count_ref, mask_ref, sems
):
    copies = [
        pltpu.make_async_copy(first_in, first_ref, sems.at[0]),
        pltpu.make_async_copy(count_in, count_ref, sems.at[1]),
        pltpu.make_async_copy(mask_in, mask_ref, sems.at[2]),
    ]
    for copy in copies:
        copy.start()
    head_size = gain_ref.shape[-1]
    kv_width = kv_heads * head_size
    join = 2 if kv_heads % 2 == 0 else 1
    span = join * head_size
    query = query_ref[...]
    mean = jnp.mean(query * query, axis=1, keepdims=True)
    normed = (query * lax.rsqrt(mean + EPSILON) * gain_ref[...]).astype(BF16)
    me = lax.axis_index(AXIS)
    size = steps * group
    row_in_tile = lax.broadcasted_iota(jnp.int32, (size, head_size), 0)
    lane = lax.broadcasted_iota(jnp.int32, (size, head_size), 1)
    stats = jnp.zeros((size, head_size), F32)
    scale = 1.0 / math.sqrt(head_size)
    blank = jnp.zeros((size, head_size), BF16)
    bases = range(0, kv_heads, join)
    scores = []
    for base in bases:
        keys = keys_ref[0, :, base * head_size : (base + join) * head_size]
        left = jnp.concatenate(
            [
                jnp.concatenate(
                    [
                        normed[(base + i) * size : (base + i + 1) * size] if i == j else blank
                        for j in range(join)
                    ],
                    axis=1,
                )
                for i in range(join)
            ],
            axis=0,
        )
        scores.append(
            lax.dot_general(left, keys, (((1,), (1,)), ((), ())), preferred_element_type=F32) * scale
        )
    tops = [jnp.max(score, axis=1, keepdims=True) for score in scores]
    weights = [jnp.exp(score - top).astype(BF16) for score, top in zip(scores, tops)]
    totals = [jnp.sum(weight.astype(F32), axis=1, keepdims=True) for weight in weights]
    for base, top, weight, total in zip(bases, tops, weights, totals):
        values = values_ref[0, :, base * head_size : (base + join) * head_size]
        mixed = jnp.dot(weight, values, preferred_element_type=F32) / total
        for i in range(join):
            h = base + i
            rows_here = slice(i * size, (i + 1) * size)
            out_ref[h * size : (h + 1) * size, :] = mixed[
                rows_here, i * head_size : (i + 1) * head_size
            ].astype(BF16)
            here = lane % kv_heads == h
            stats = jnp.where(
                here, jnp.where(lane < 3 * kv_heads, top[rows_here], total[rows_here]), stats
            )
    for copy in copies:
        copy.wait()
    rows = first_ref.shape[0]

    def find(row, carry):
        owner, tile = carry
        offset = me - first_ref[row]
        inside = (offset >= 0) & (offset < count_ref[row])
        return jnp.where(inside, row, owner), jnp.where(inside, offset, tile)

    owner, tile = lax.fori_loop(0, rows, find, (jnp.int32(0), jnp.int32(0)), unroll=rows <= 16)
    live = jnp.zeros((size, head_size), jnp.bool_)
    for s in range(steps):
        alive = (tile == 0) | (mask_ref[owner, s, tile] == 1)
        live = live | ((row_in_tile // group == s) & alive)
    stats = jnp.where(live | (lane >= 3 * kv_heads), stats, NEGATIVE_FLOOR)
    high = stats.astype(BF16).astype(F32)
    rest = stats - high
    middle = rest.astype(BF16).astype(F32)
    low = rest - middle
    piece = (lane // kv_heads) % 3
    packed = jnp.where(piece == 0, high, jnp.where(piece == 1, middle, low))
    out_ref[kv_heads * size :, :] = packed.astype(BF16)


def finish_kernel(
    order, kv_heads, group, steps, max_tiles, gate_ref, first_ref, count_ref, tiles_ref, weight_ref,
    out_ref, stats, turned
):
    rows = first_ref.shape[0]
    head_size = tiles_ref.shape[-1]
    size = steps * group
    block = (kv_heads + 1) * size
    slots = tiles_ref.shape[0]
    me = lax.axis_index(AXIS)
    packed = tiles_ref[:, kv_heads * size :, :].astype(F32).reshape(slots * size, head_size)
    whole = (
        packed
        + pltpu.roll(packed, head_size - kv_heads, 1)
        + pltpu.roll(packed, head_size - 2 * kv_heads, 1)
    )
    stats[0] = whole
    stats[1] = pltpu.roll(whole, head_size - 3 * kv_heads, 1)
    first = first_ref[...].reshape(1, rows)
    count = count_ref[...].reshape(1, rows)
    pairs = rows * steps
    masks = [order.index(1 << i) for i in range(slots.bit_length() - 1)]

    def one_row(row, carry):
        here = (lax.broadcasted_iota(jnp.int32, (1, rows), 1) == row).astype(jnp.int32)
        begin = jnp.sum(first * here)
        length = jnp.sum(count * here)
        places = [
            combine_bits(me ^ (begin + jnp.minimum(k, length - 1)), masks) for k in range(max_tiles)
        ]
        tops = []
        for k in range(max_tiles):
            top = stats[0, pl.ds(places[k] * size, size), :]
            tops.append(jnp.where(k < length, top, NEGATIVE_FLOOR))
        best = functools.reduce(jnp.maximum, tops)
        factors = []
        for k in range(max_tiles):
            total = stats[1, pl.ds(places[k] * size, size), :]
            factor = jnp.exp(tops[k] - best) * total
            factors.append(jnp.where(tops[k] > 0.5 * NEGATIVE_FLOOR, factor, 0.0))
        denominator = functools.reduce(jnp.add, factors)
        shares = [factor / denominator for factor in factors]
        for h in range(kv_heads):
            mixed = jnp.zeros((size, head_size), F32)
            for k in range(max_tiles):
                value = tiles_ref[places[k], h * size : (h + 1) * size, :].astype(F32)
                mixed = mixed + shares[k][:, h : h + 1] * value
            for s in range(steps):
                turned[pl.ds(h * group * pairs + row * steps + s, group, stride=pairs), :] = mixed[
                    s * group : (s + 1) * group
                ]
        return carry

    lax.fori_loop(0, rows, one_row, 0, unroll=8)
    total = jnp.zeros((pairs, weight_ref.shape[1]), F32)
    for h in range(kv_heads):
        left = jnp.concatenate(
            [
                turned[(h * group + g) * pairs : (h * group + g + 1) * pairs, :].astype(BF16)
                for g in range(group)
            ],
            axis=1,
        )
        span = group * head_size
        total = total + jnp.dot(
            left, weight_ref[h * span : (h + 1) * span, :], preferred_element_type=F32
        )
    gate = gate_ref[:1, :1]
    result = (total * gate).astype(BF16)
    out_ref[...] = result.reshape(rows, steps, result.shape[1])


def body(
    devices,
    normed_input,
    query_weight,
    query_gain,
    image_cache,
    tile_count,
    image_first_slot,
    cross_tile_mask,
    output_weight,
    output_gate,
):
    rows, steps, depth = normed_input.shape
    head_size = query_gain.shape[0]
    width = query_weight.shape[1]
    heads = width // head_size
    kv_heads = image_cache.shape[2] // (2 * head_size)
    group = heads // kv_heads
    tile_rows = steps * heads
    stages = exchange_stages(devices.bit_length() - 1)
    order = positions(stages)
    half = devices // 2
    chunks = 4
    keep, send = pl.pallas_call(
        functools.partial(project_kernel, order, chunks, kv_heads, group, head_size),
        out_shape=[struct((half * tile_rows, head_size), F32)] * 2,
        in_specs=[HBM] * 4,
        out_specs=[VMEM, VMEM],
        scratch_shapes=[
            pltpu.VMEM((depth, width), BF16),
            pltpu.VMEM(normed_input.shape, BF16),
            pltpu.SMEM(image_first_slot.shape, jnp.int32),
            pltpu.SMEM(tile_count.shape, jnp.int32),
            pltpu.SemaphoreType.DMA((chunks,)),
            pltpu.SemaphoreType.DMA((3,)),
        ],
        compiler_params=params(12),
    )(*[in_hbm(x) for x in (normed_input, query_weight, image_first_slot, tile_count)])
    total = keep + exchange(send, 1, devices)
    cache = []
    for group_bits in stages[1:]:
        steps_out = offsets(group_bits)
        size = total.shape[0] // len(steps_out)
        pieces = [total[i * size : (i + 1) * size] for i in range(len(steps_out))]
        sent = pieces[1:]
        got = [exchange(piece, step, devices) for piece, step in zip(sent, steps_out[1:])]
        if len(cache) < 2:
            half, pieces[0], gate = fetch(image_cache, len(cache), pieces[0], output_gate)
            cache.append(half)
        total = functools.reduce(jnp.add, [pieces[0]] + got)
    block = (kv_heads + 1) * steps * group
    tile = pl.pallas_call(
        functools.partial(attend_kernel, kv_heads, group, steps),
        out_shape=struct((block, head_size), BF16),
        in_specs=[VMEM] * 7,
        out_specs=VMEM,
        scratch_shapes=[
            pltpu.SMEM(image_first_slot.shape, jnp.int32),
            pltpu.SMEM(tile_count.shape, jnp.int32),
            pltpu.SMEM(cross_tile_mask.shape, jnp.int32),
            pltpu.SemaphoreType.DMA((3,)),
        ],
        compiler_params=params(6),
    )(total, query_gain, *cache, image_first_slot, tile_count, cross_tile_mask)
    gathered = tile[None]
    for group_bits in reversed(stages):
        gathered = jnp.concatenate(
            [gathered] + [exchange(gathered, step, devices) for step in offsets(group_bits)[1:]], axis=0
        )
    scratch = 4 * head_size * (2 * devices * steps * group + heads * rows * steps)
    return pl.pallas_call(
        functools.partial(finish_kernel, order, kv_heads, group, steps, cross_tile_mask.shape[2]),
        out_shape=struct((rows, steps, output_weight.shape[1]), BF16),
        in_specs=[VMEM] * 5,
        out_specs=VMEM,
        scratch_shapes=[
            pltpu.VMEM((2, devices * steps * group, head_size), F32),
            pltpu.VMEM((heads * rows * steps, head_size), F32),
        ],
        compiler_params=params(6 + (2 * scratch >> 20)),
    )(gate, image_first_slot, tile_count, gathered, output_weight)


def solution(mesh):
    return jax.shard_map(
        functools.partial(body, mesh.shape[AXIS]),
        mesh=mesh,
        in_specs=(
            P("groups", None, "tensor"),
            P("tensor", None),
            P(),
            P(("groups", "tensor"), None, None),
            P("groups"),
            P("groups"),
            P("groups", None, None),
            P(None, "tensor"),
            P(),
        ),
        out_specs=P("groups", None, "tensor"),
        check_vma=False,
    )
```

```python
import functools
import math

import jax
import jax.numpy as jnp
from jax import lax
from jax.experimental import pallas as pl
from jax.experimental.pallas import tpu as pltpu
from jax.sharding import PartitionSpec as P

EPSILON = 1e-05
NEGATIVE_FLOOR = -1e30
AXIS = "tensor"
F32 = jnp.float32
BF16 = jnp.bfloat16
VMEM = pl.BlockSpec(memory_space=pltpu.VMEM)
SMEM = pl.BlockSpec(memory_space=pltpu.SMEM)
ANY = pl.BlockSpec(memory_space=pl.ANY)
HBM = pl.BlockSpec(memory_space=pltpu.HBM)


def struct(shape, dtype):
    return jax.ShapeDtypeStruct(shape, dtype)


def in_hbm(array):
    return pltpu.with_memory_space_constraint(array, pltpu.HBM)


def params(mebibytes):
    return pltpu.CompilerParams(vmem_limit_bytes=mebibytes << 20)


def exchange_stages(bits, square):
    if bits < 3:
        return [[1 << bit] for bit in range(bits)]
    return [[1], square] + [[(1 << bit) | 1] for bit in range(3, bits)]


def offsets(group):
    result = [0]
    for difference in group:
        result = result + [other ^ difference for other in result]
    return result


def positions(stages):
    result = [0]
    for group in stages:
        result = [base ^ step for base in result for step in offsets(group)]
    return result


def combine_bits(value, masks):
    result = value & 0
    for bit, mask in enumerate(masks):
        result = result ^ (((value >> bit) & 1) * mask)
    return result


def exchange(array, difference, count):
    return lax.ppermute(array, AXIS, [(i, i ^ difference) for i in range(count)])


def project_kernel(
    order, chunks, kv_heads, group, head_size, x_hbm, weight_hbm, first_hbm, count_hbm, keep_ref,
    send_ref, weight, x_ref, first_ref, count_ref, sems, small_sems
):
    rows, steps, depth = x_ref.shape
    width = weight.shape[1]
    chunk = width // chunks
    small = [
        pltpu.make_async_copy(source, target, small_sems.at[i])
        for i, (source, target) in enumerate(
            [(x_hbm, x_ref), (first_hbm, first_ref), (count_hbm, count_ref)]
        )
    ]
    for copy in small:
        copy.start()
    copies = [
        pltpu.make_async_copy(
            weight_hbm.at[:, pl.ds(c * chunk, chunk)], weight.at[:, pl.ds(c * chunk, chunk)], sems.at[c]
        )
        for c in range(chunks)
    ]
    for copy in copies:
        copy.start()
    for copy in small:
        copy.wait()
    slots = len(order)
    half = slots // 2
    me = lax.axis_index(AXIS)
    shape = (steps * slots, rows * steps)
    out_row = lax.broadcasted_iota(jnp.int32, shape, 0)
    place = out_row % slots
    step = out_row // slots
    in_row = lax.broadcasted_iota(jnp.int32, shape, 1)
    slot = combine_bits(place, [order[1 << i] for i in range(slots.bit_length() - 1)]) ^ me
    start = jnp.zeros(shape, jnp.int32)
    length = jnp.zeros(shape, jnp.int32)
    for row in range(rows):
        here = in_row // steps == row
        start = jnp.where(here, first_ref[row], start)
        length = jnp.where(here, count_ref[row], length)
    chosen = (slot >= start) & (slot < start + length) & (in_row % steps == step)
    flat = x_ref[...].reshape(rows * steps, depth)
    picked = jnp.dot(
        jnp.where(chosen, 1.0, 0.0).astype(BF16), flat, preferred_element_type=F32
    ).astype(BF16)
    tile_rows = steps * kv_heads * group
    heads_per_chunk = chunk // head_size
    for c in range(chunks):
        copies[c].wait()
        result = jnp.dot(
            picked, weight[:, c * chunk : (c + 1) * chunk], preferred_element_type=F32
        )
        for local in range(heads_per_chunk):
            head = c * heads_per_chunk + local
            for s in range(steps):
                at = (head // group) * steps * group + s * group + head % group
                block = result[s * slots : (s + 1) * slots, local * head_size : (local + 1) * head_size]
                keep_ref[pl.ds(at, half, stride=tile_rows), :] = block[:half]
                send_ref[pl.ds(at, half, stride=tile_rows), :] = block[half:]


def fetch_kernel(part, cache_hbm, before_ref, gate_ref, cache_ref, after_ref, tanh_ref, sems):
    del before_ref, after_ref
    pieces = sems.shape[0]
    span = cache_ref.shape[2] // pieces
    copies = [
        pltpu.make_async_copy(
            cache_hbm.at[:, :, pl.ds((part * pieces + i) * span, span)],
            cache_ref.at[:, :, pl.ds(i * span, span)],
            sems.at[i],
        )
        for i in range(pieces)
    ]
    for copy in copies:
        copy.start()
    tanh_ref[...] = jnp.tanh(jnp.full(tanh_ref.shape, gate_ref[0], F32))
    for copy in copies:
        copy.wait()


def fetch(cache, part, held, gate):
    return pl.pallas_call(
        functools.partial(fetch_kernel, part),
        out_shape=[
            struct((*cache.shape[:2], cache.shape[2] // 2), cache.dtype),
            struct(held.shape, held.dtype),
            struct((8, 128), F32),
        ],
        in_specs=[HBM, ANY, SMEM],
        out_specs=[VMEM, ANY, VMEM],
        scratch_shapes=[pltpu.SemaphoreType.DMA((4,))],
        input_output_aliases={1: 1},
        compiler_params=params(1),
        cost_estimate=pl.CostEstimate(flops=0, bytes_accessed=cache.size, transcendentals=0),
    )(in_hbm(cache), held, gate)


def attend_kernel(
    kv_heads, group, steps, query_ref, gain_ref, keys_ref, values_ref, first_in, count_in, mask_in,
    out_ref, first_ref, count_ref, mask_ref, sems
):
    copies = [
        pltpu.make_async_copy(first_in, first_ref, sems.at[0]),
        pltpu.make_async_copy(count_in, count_ref, sems.at[1]),
        pltpu.make_async_copy(mask_in, mask_ref, sems.at[2]),
    ]
    for copy in copies:
        copy.start()
    head_size = gain_ref.shape[-1]
    kv_width = kv_heads * head_size
    join = 2 if kv_heads % 2 == 0 else 1
    span = join * head_size
    query = query_ref[...]
    mean = jnp.mean(query * query, axis=1, keepdims=True)
    normed = (query * lax.rsqrt(mean + EPSILON) * gain_ref[...]).astype(BF16)
    me = lax.axis_index(AXIS)
    size = steps * group
    row_in_tile = lax.broadcasted_iota(jnp.int32, (size, head_size), 0)
    lane = lax.broadcasted_iota(jnp.int32, (size, head_size), 1)
    stats = jnp.zeros((size, head_size), F32)
    scale = 1.0 / math.sqrt(head_size)
    blank = jnp.zeros((size, head_size), BF16)
    bases = range(0, kv_heads, join)
    scores = []
    for base in bases:
        keys = keys_ref[0, :, base * head_size : (base + join) * head_size]
        left = jnp.concatenate(
            [
                jnp.concatenate(
                    [
                        normed[(base + i) * size : (base + i + 1) * size] if i == j else blank
                        for j in range(join)
                    ],
                    axis=1,
                )
                for i in range(join)
            ],
            axis=0,
        )
        scores.append(
            lax.dot_general(left, keys, (((1,), (1,)), ((), ())), preferred_element_type=F32) * scale
        )
    tops = [jnp.max(score, axis=1, keepdims=True) for score in scores]
    weights = [jnp.exp(score - top).astype(BF16) for score, top in zip(scores, tops)]
    totals = [jnp.sum(weight.astype(F32), axis=1, keepdims=True) for weight in weights]
    for base, top, weight, total in zip(bases, tops, weights, totals):
        values = values_ref[0, :, base * head_size : (base + join) * head_size]
        mixed = jnp.dot(weight, values, preferred_element_type=F32) / total
        for i in range(join):
            h = base + i
            rows_here = slice(i * size, (i + 1) * size)
            out_ref[h * size : (h + 1) * size, :] = mixed[
                rows_here, i * head_size : (i + 1) * head_size
            ].astype(BF16)
            here = lane % kv_heads == h
            stats = jnp.where(
                here, jnp.where(lane < 3 * kv_heads, top[rows_here], total[rows_here]), stats
            )
    for copy in copies:
        copy.wait()
    rows = first_ref.shape[0]

    def find(row, carry):
        owner, tile = carry
        offset = me - first_ref[row]
        inside = (offset >= 0) & (offset < count_ref[row])
        return jnp.where(inside, row, owner), jnp.where(inside, offset, tile)

    owner, tile = lax.fori_loop(0, rows, find, (jnp.int32(0), jnp.int32(0)), unroll=rows <= 16)
    live = jnp.zeros((size, head_size), jnp.bool_)
    for s in range(steps):
        alive = (tile == 0) | (mask_ref[owner, s, tile] == 1)
        live = live | ((row_in_tile // group == s) & alive)
    stats = jnp.where(live | (lane >= 3 * kv_heads), stats, NEGATIVE_FLOOR)
    high = stats.astype(BF16).astype(F32)
    rest = stats - high
    middle = rest.astype(BF16).astype(F32)
    low = rest - middle
    piece = (lane // kv_heads) % 3
    packed = jnp.where(piece == 0, high, jnp.where(piece == 1, middle, low))
    out_ref[kv_heads * size :, :] = packed.astype(BF16)


def finish_kernel(
    order, kv_heads, group, steps, max_tiles, gate_ref, first_ref, count_ref, tiles_ref, weight_ref,
    out_ref, stats, turned
):
    rows = first_ref.shape[0]
    head_size = tiles_ref.shape[-1]
    size = steps * group
    block = (kv_heads + 1) * size
    slots = tiles_ref.shape[0]
    me = lax.axis_index(AXIS)
    packed = tiles_ref[:, kv_heads * size :, :].astype(F32).reshape(slots * size, head_size)
    whole = (
        packed
        + pltpu.roll(packed, head_size - kv_heads, 1)
        + pltpu.roll(packed, head_size - 2 * kv_heads, 1)
    )
    stats[0] = whole
    stats[1] = pltpu.roll(whole, head_size - 3 * kv_heads, 1)
    first = first_ref[...].reshape(1, rows)
    count = count_ref[...].reshape(1, rows)
    pairs = rows * steps
    masks = [order.index(1 << i) for i in range(slots.bit_length() - 1)]

    def one_row(row, carry):
        here = (lax.broadcasted_iota(jnp.int32, (1, rows), 1) == row).astype(jnp.int32)
        begin = jnp.sum(first * here)
        length = jnp.sum(count * here)
        places = [
            combine_bits(me ^ (begin + jnp.minimum(k, length - 1)), masks) for k in range(max_tiles)
        ]
        tops = []
        for k in range(max_tiles):
            top = stats[0, pl.ds(places[k] * size, size), :]
            tops.append(jnp.where(k < length, top, NEGATIVE_FLOOR))
        best = functools.reduce(jnp.maximum, tops)
        factors = []
        for k in range(max_tiles):
            total = stats[1, pl.ds(places[k] * size, size), :]
            factor = jnp.exp(tops[k] - best) * total
            factors.append(jnp.where(tops[k] > 0.5 * NEGATIVE_FLOOR, factor, 0.0))
        denominator = functools.reduce(jnp.add, factors)
        shares = [factor / denominator for factor in factors]
        for h in range(kv_heads):
            mixed = jnp.zeros((size, head_size), F32)
            for k in range(max_tiles):
                value = tiles_ref[places[k], h * size : (h + 1) * size, :].astype(F32)
                mixed = mixed + shares[k][:, h : h + 1] * value
            for s in range(steps):
                turned[pl.ds(h * group * pairs + row * steps + s, group, stride=pairs), :] = mixed[
                    s * group : (s + 1) * group
                ]
        return carry

    lax.fori_loop(0, rows, one_row, 0, unroll=8)
    total = jnp.zeros((pairs, weight_ref.shape[1]), F32)
    for h in range(kv_heads):
        left = jnp.concatenate(
            [
                turned[(h * group + g) * pairs : (h * group + g + 1) * pairs, :].astype(BF16)
                for g in range(group)
            ],
            axis=1,
        )
        span = group * head_size
        total = total + jnp.dot(
            left, weight_ref[h * span : (h + 1) * span, :], preferred_element_type=F32
        )
    gate = gate_ref[:1, :1]
    result = (total * gate).astype(BF16)
    out_ref[...] = result.reshape(rows, steps, result.shape[1])


def body(
    devices,
    normed_input,
    query_weight,
    query_gain,
    image_cache,
    tile_count,
    image_first_slot,
    cross_tile_mask,
    output_weight,
    output_gate,
):
    rows, steps, depth = normed_input.shape
    head_size = query_gain.shape[0]
    width = query_weight.shape[1]
    heads = width // head_size
    kv_heads = image_cache.shape[2] // (2 * head_size)
    group = heads // kv_heads
    tile_rows = steps * heads
    stages = exchange_stages(devices.bit_length() - 1, [4, 2])
    order = positions(stages)
    half = devices // 2
    chunks = 4
    keep, send = pl.pallas_call(
        functools.partial(project_kernel, order, chunks, kv_heads, group, head_size),
        out_shape=[struct((half * tile_rows, head_size), F32)] * 2,
        in_specs=[HBM] * 4,
        out_specs=[VMEM, VMEM],
        scratch_shapes=[
            pltpu.VMEM((depth, width), BF16),
            pltpu.VMEM(normed_input.shape, BF16),
            pltpu.SMEM(image_first_slot.shape, jnp.int32),
            pltpu.SMEM(tile_count.shape, jnp.int32),
            pltpu.SemaphoreType.DMA((chunks,)),
            pltpu.SemaphoreType.DMA((3,)),
        ],
        compiler_params=params(12),
    )(*[in_hbm(x) for x in (normed_input, query_weight, image_first_slot, tile_count)])
    total = keep + exchange(send, 1, devices)
    cache = []
    for group_bits in stages[1:]:
        steps_out = offsets(group_bits)
        size = total.shape[0] // len(steps_out)
        pieces = [total[i * size : (i + 1) * size] for i in range(len(steps_out))]
        sent = pieces[1:]
        got = [exchange(piece, step, devices) for piece, step in zip(sent, steps_out[1:])]
        if len(cache) < 2:
            half, pieces[0], gate = fetch(image_cache, len(cache), pieces[0], output_gate)
            cache.append(half)
        total = functools.reduce(jnp.add, [pieces[0]] + got)
    block = (kv_heads + 1) * steps * group
    tile = pl.pallas_call(
        functools.partial(attend_kernel, kv_heads, group, steps),
        out_shape=struct((block, head_size), BF16),
        in_specs=[VMEM] * 7,
        out_specs=VMEM,
        scratch_shapes=[
            pltpu.SMEM(image_first_slot.shape, jnp.int32),
            pltpu.SMEM(tile_count.shape, jnp.int32),
            pltpu.SMEM(cross_tile_mask.shape, jnp.int32),
            pltpu.SemaphoreType.DMA((3,)),
        ],
        compiler_params=params(6),
    )(total, query_gain, *cache, image_first_slot, tile_count, cross_tile_mask)
    stages = exchange_stages(devices.bit_length() - 1, [4, 3])
    order = positions(stages)
    gathered = tile[None]
    for group_bits in reversed(stages):
        gathered = jnp.concatenate(
            [gathered] + [exchange(gathered, step, devices) for step in offsets(group_bits)[1:]], axis=0
        )
    scratch = 4 * head_size * (2 * devices * steps * group + heads * rows * steps)
    return pl.pallas_call(
        functools.partial(finish_kernel, order, kv_heads, group, steps, cross_tile_mask.shape[2]),
        out_shape=struct((rows, steps, output_weight.shape[1]), BF16),
        in_specs=[VMEM] * 5,
        out_specs=VMEM,
        scratch_shapes=[
            pltpu.VMEM((2, devices * steps * group, head_size), F32),
            pltpu.VMEM((heads * rows * steps, head_size), F32),
        ],
        compiler_params=params(6 + (2 * scratch >> 20)),
    )(gate, image_first_slot, tile_count, gathered, output_weight)


def solution(mesh):
    return jax.shard_map(
        functools.partial(body, mesh.shape[AXIS]),
        mesh=mesh,
        in_specs=(
            P("groups", None, "tensor"),
            P("tensor", None),
            P(),
            P(("groups", "tensor"), None, None),
            P("groups"),
            P("groups"),
            P("groups", None, None),
            P(None, "tensor"),
            P(),
        ),
        out_specs=P("groups", None, "tensor"),
        check_vma=False,
    )
```

```python
import functools
import math

import jax
import jax.numpy as jnp
from jax import lax
from jax.experimental import pallas as pl
from jax.experimental.pallas import tpu as pltpu
from jax.sharding import PartitionSpec as P

EPSILON = 1e-05
NEGATIVE_FLOOR = -1e30
AXIS = "tensor"
F32 = jnp.float32
BF16 = jnp.bfloat16
VMEM = pl.BlockSpec(memory_space=pltpu.VMEM)
SMEM = pl.BlockSpec(memory_space=pltpu.SMEM)
ANY = pl.BlockSpec(memory_space=pl.ANY)
HBM = pl.BlockSpec(memory_space=pltpu.HBM)


def struct(shape, dtype):
    return jax.ShapeDtypeStruct(shape, dtype)


def in_hbm(array):
    return pltpu.with_memory_space_constraint(array, pltpu.HBM)


def params(mebibytes):
    return pltpu.CompilerParams(vmem_limit_bytes=mebibytes << 20)


def exchange_stages(bits, square):
    if bits < 3:
        return [[1 << bit] for bit in range(bits)]
    return [[1], square] + [[(1 << bit) | 1] for bit in range(3, bits)]


def offsets(group):
    result = [0]
    for difference in group:
        result = result + [other ^ difference for other in result]
    return result


def positions(stages):
    result = [0]
    for group in stages:
        result = [base ^ step for base in result for step in offsets(group)]
    return result


def combine_bits(value, masks):
    result = value & 0
    for bit, mask in enumerate(masks):
        result = result ^ (((value >> bit) & 1) * mask)
    return result


def exchange(array, difference, count):
    return lax.ppermute(array, AXIS, [(i, i ^ difference) for i in range(count)])


def project_kernel(
    order, chunks, kv_heads, group, head_size, x_hbm, weight_hbm, first_hbm, count_hbm, keep_ref,
    send_ref, weight, x_ref, first_ref, count_ref, sems, small_sems
):
    rows, steps, depth = x_ref.shape
    width = weight.shape[1]
    chunk = width // chunks
    small = [
        pltpu.make_async_copy(source, target, small_sems.at[i])
        for i, (source, target) in enumerate(
            [(x_hbm, x_ref), (first_hbm, first_ref), (count_hbm, count_ref)]
        )
    ]
    for copy in small:
        copy.start()
    copies = [
        pltpu.make_async_copy(
            weight_hbm.at[:, pl.ds(c * chunk, chunk)], weight.at[:, pl.ds(c * chunk, chunk)], sems.at[c]
        )
        for c in range(chunks)
    ]
    for copy in copies:
        copy.start()
    for copy in small:
        copy.wait()
    slots = len(order)
    half = slots // 2
    me = lax.axis_index(AXIS)
    shape = (steps * slots, rows * steps)
    out_row = lax.broadcasted_iota(jnp.int32, shape, 0)
    place = out_row % slots
    step = out_row // slots
    in_row = lax.broadcasted_iota(jnp.int32, shape, 1)
    slot = combine_bits(place, [order[1 << i] for i in range(slots.bit_length() - 1)]) ^ me
    start = jnp.zeros(shape, jnp.int32)
    length = jnp.zeros(shape, jnp.int32)
    for row in range(rows):
        here = in_row // steps == row
        start = jnp.where(here, first_ref[row], start)
        length = jnp.where(here, count_ref[row], length)
    chosen = (slot >= start) & (slot < start + length) & (in_row % steps == step)
    flat = x_ref[...].reshape(rows * steps, depth)
    picked = jnp.dot(
        jnp.where(chosen, 1.0, 0.0).astype(BF16), flat, preferred_element_type=F32
    ).astype(BF16)
    tile_rows = steps * kv_heads * group
    heads_per_chunk = chunk // head_size
    for c in range(chunks):
        copies[c].wait()
        result = jnp.dot(
            picked, weight[:, c * chunk : (c + 1) * chunk], preferred_element_type=F32
        )
        for local in range(heads_per_chunk):
            head = c * heads_per_chunk + local
            for s in range(steps):
                at = (head // group) * steps * group + s * group + head % group
                block = result[s * slots : (s + 1) * slots, local * head_size : (local + 1) * head_size]
                keep_ref[pl.ds(at, half, stride=tile_rows), :] = block[:half]
                send_ref[pl.ds(at, half, stride=tile_rows), :] = block[half:]


def fetch_kernel(part, cache_hbm, before_ref, gate_ref, cache_ref, after_ref, tanh_ref, sems):
    del before_ref, after_ref
    pieces = sems.shape[0]
    span = cache_ref.shape[2] // pieces
    copies = [
        pltpu.make_async_copy(
            cache_hbm.at[:, :, pl.ds((part * pieces + i) * span, span)],
            cache_ref.at[:, :, pl.ds(i * span, span)],
            sems.at[i],
        )
        for i in range(pieces)
    ]
    for copy in copies:
        copy.start()
    tanh_ref[...] = jnp.tanh(jnp.full(tanh_ref.shape, gate_ref[0], F32))
    for copy in copies:
        copy.wait()


def fetch(cache, part, held, gate):
    return pl.pallas_call(
        functools.partial(fetch_kernel, part),
        out_shape=[
            struct((*cache.shape[:2], cache.shape[2] // 2), cache.dtype),
            struct(held.shape, held.dtype),
            struct((8, 128), F32),
        ],
        in_specs=[HBM, ANY, SMEM],
        out_specs=[VMEM, ANY, VMEM],
        scratch_shapes=[pltpu.SemaphoreType.DMA((4,))],
        input_output_aliases={1: 1},
        compiler_params=params(1),
        cost_estimate=pl.CostEstimate(flops=0, bytes_accessed=cache.size, transcendentals=0),
    )(in_hbm(cache), held, gate)


def attend_kernel(
    kv_heads, group, steps, query_ref, gain_ref, keys_ref, values_ref, first_in, count_in, mask_in,
    out_ref, first_ref, count_ref, mask_ref, sems
):
    copies = [
        pltpu.make_async_copy(first_in, first_ref, sems.at[0]),
        pltpu.make_async_copy(count_in, count_ref, sems.at[1]),
        pltpu.make_async_copy(mask_in, mask_ref, sems.at[2]),
    ]
    for copy in copies:
        copy.start()
    head_size = gain_ref.shape[-1]
    kv_width = kv_heads * head_size
    join = 2 if kv_heads % 2 == 0 else 1
    span = join * head_size
    query = query_ref[...]
    mean = jnp.mean(query * query, axis=1, keepdims=True)
    normed = (query * lax.rsqrt(mean + EPSILON) * gain_ref[...]).astype(BF16)
    me = lax.axis_index(AXIS)
    size = steps * group
    row_in_tile = lax.broadcasted_iota(jnp.int32, (size, head_size), 0)
    lane = lax.broadcasted_iota(jnp.int32, (size, head_size), 1)
    stats = jnp.zeros((size, head_size), F32)
    scale = 1.0 / math.sqrt(head_size)
    blank = jnp.zeros((size, head_size), BF16)
    bases = range(0, kv_heads, join)
    scores = []
    for base in bases:
        keys = keys_ref[0, :, base * head_size : (base + join) * head_size]
        left = jnp.concatenate(
            [
                jnp.concatenate(
                    [
                        normed[(base + i) * size : (base + i + 1) * size] if i == j else blank
                        for j in range(join)
                    ],
                    axis=1,
                )
                for i in range(join)
            ],
            axis=0,
        )
        scores.append(
            lax.dot_general(left, keys, (((1,), (1,)), ((), ())), preferred_element_type=F32)
        )
    tops = [jnp.max(score, axis=1, keepdims=True) for score in scores]
    weights = [
        jnp.exp2((score - top) * (scale * math.log2(math.e))).astype(BF16)
        for score, top in zip(scores, tops)
    ]
    tops = [top * scale for top in tops]
    totals = [jnp.sum(weight.astype(F32), axis=1, keepdims=True) for weight in weights]
    for base, top, weight, total in zip(bases, tops, weights, totals):
        values = values_ref[0, :, base * head_size : (base + join) * head_size]
        mixed = jnp.dot(weight, values, preferred_element_type=F32) / total
        for i in range(join):
            h = base + i
            rows_here = slice(i * size, (i + 1) * size)
            out_ref[h * size : (h + 1) * size, :] = mixed[
                rows_here, i * head_size : (i + 1) * head_size
            ].astype(BF16)
            here = lane % kv_heads == h
            stats = jnp.where(
                here, jnp.where(lane < 3 * kv_heads, top[rows_here], total[rows_here]), stats
            )
    for copy in copies:
        copy.wait()
    rows = first_ref.shape[0]

    def find(row, carry):
        owner, tile = carry
        offset = me - first_ref[row]
        inside = (offset >= 0) & (offset < count_ref[row])
        return jnp.where(inside, row, owner), jnp.where(inside, offset, tile)

    owner, tile = lax.fori_loop(0, rows, find, (jnp.int32(0), jnp.int32(0)), unroll=rows <= 16)
    live = jnp.zeros((size, head_size), jnp.bool_)
    for s in range(steps):
        alive = (tile == 0) | (mask_ref[owner, s, tile] == 1)
        live = live | ((row_in_tile // group == s) & alive)
    stats = jnp.where(live | (lane >= 3 * kv_heads), stats, NEGATIVE_FLOOR)
    high = stats.astype(BF16).astype(F32)
    rest = stats - high
    middle = rest.astype(BF16).astype(F32)
    low = rest - middle
    piece = (lane // kv_heads) % 3
    packed = jnp.where(piece == 0, high, jnp.where(piece == 1, middle, low))
    out_ref[kv_heads * size :, :] = packed.astype(BF16)


def finish_kernel(
    order, kv_heads, group, steps, max_tiles, gate_ref, first_ref, count_ref, tiles_ref, weight_ref,
    out_ref, stats, turned
):
    rows = first_ref.shape[0]
    head_size = tiles_ref.shape[-1]
    size = steps * group
    block = (kv_heads + 1) * size
    slots = tiles_ref.shape[0]
    me = lax.axis_index(AXIS)
    packed = tiles_ref[:, kv_heads * size :, :].astype(F32).reshape(slots * size, head_size)
    whole = (
        packed
        + pltpu.roll(packed, head_size - kv_heads, 1)
        + pltpu.roll(packed, head_size - 2 * kv_heads, 1)
    )
    stats[0] = whole
    stats[1] = pltpu.roll(whole, head_size - 3 * kv_heads, 1)
    first = first_ref[...].reshape(1, rows)
    count = count_ref[...].reshape(1, rows)
    pairs = rows * steps
    masks = [order.index(1 << i) for i in range(slots.bit_length() - 1)]

    def one_row(row, carry):
        here = (lax.broadcasted_iota(jnp.int32, (1, rows), 1) == row).astype(jnp.int32)
        begin = jnp.sum(first * here)
        length = jnp.sum(count * here)
        places = [
            combine_bits(me ^ (begin + jnp.minimum(k, length - 1)), masks) for k in range(max_tiles)
        ]
        tops = []
        for k in range(max_tiles):
            top = stats[0, pl.ds(places[k] * size, size), :]
            tops.append(jnp.where(k < length, top, NEGATIVE_FLOOR))
        best = functools.reduce(jnp.maximum, tops)
        factors = []
        for k in range(max_tiles):
            total = stats[1, pl.ds(places[k] * size, size), :]
            factor = jnp.exp(tops[k] - best) * total
            factors.append(jnp.where(tops[k] > 0.5 * NEGATIVE_FLOOR, factor, 0.0))
        denominator = functools.reduce(jnp.add, factors)
        shares = [factor / denominator for factor in factors]
        for h in range(kv_heads):
            mixed = jnp.zeros((size, head_size), F32)
            for k in range(max_tiles):
                value = tiles_ref[places[k], h * size : (h + 1) * size, :].astype(F32)
                mixed = mixed + shares[k][:, h : h + 1] * value
            for s in range(steps):
                turned[pl.ds(h * group * pairs + row * steps + s, group, stride=pairs), :] = mixed[
                    s * group : (s + 1) * group
                ]
        return carry

    lax.fori_loop(0, rows, one_row, 0, unroll=8)
    total = jnp.zeros((pairs, weight_ref.shape[1]), F32)
    for h in range(kv_heads):
        left = jnp.concatenate(
            [
                turned[(h * group + g) * pairs : (h * group + g + 1) * pairs, :].astype(BF16)
                for g in range(group)
            ],
            axis=1,
        )
        span = group * head_size
        total = total + jnp.dot(
            left, weight_ref[h * span : (h + 1) * span, :], preferred_element_type=F32
        )
    gate = gate_ref[:1, :1]
    result = (total * gate).astype(BF16)
    out_ref[...] = result.reshape(rows, steps, result.shape[1])


def body(
    devices,
    normed_input,
    query_weight,
    query_gain,
    image_cache,
    tile_count,
    image_first_slot,
    cross_tile_mask,
    output_weight,
    output_gate,
):
    rows, steps, depth = normed_input.shape
    head_size = query_gain.shape[0]
    width = query_weight.shape[1]
    heads = width // head_size
    kv_heads = image_cache.shape[2] // (2 * head_size)
    group = heads // kv_heads
    tile_rows = steps * heads
    stages = exchange_stages(devices.bit_length() - 1, [4, 2])
    order = positions(stages)
    half = devices // 2
    chunks = 4
    keep, send = pl.pallas_call(
        functools.partial(project_kernel, order, chunks, kv_heads, group, head_size),
        out_shape=[struct((half * tile_rows, head_size), F32)] * 2,
        in_specs=[HBM] * 4,
        out_specs=[VMEM, VMEM],
        scratch_shapes=[
            pltpu.VMEM((depth, width), BF16),
            pltpu.VMEM(normed_input.shape, BF16),
            pltpu.SMEM(image_first_slot.shape, jnp.int32),
            pltpu.SMEM(tile_count.shape, jnp.int32),
            pltpu.SemaphoreType.DMA((chunks,)),
            pltpu.SemaphoreType.DMA((3,)),
        ],
        compiler_params=params(12),
    )(*[in_hbm(x) for x in (normed_input, query_weight, image_first_slot, tile_count)])
    total = keep + exchange(send, 1, devices)
    cache = []
    for group_bits in stages[1:]:
        steps_out = offsets(group_bits)
        size = total.shape[0] // len(steps_out)
        pieces = [total[i * size : (i + 1) * size] for i in range(len(steps_out))]
        sent = pieces[1:]
        got = [exchange(piece, step, devices) for piece, step in zip(sent, steps_out[1:])]
        if len(cache) < 2:
            half, pieces[0], gate = fetch(image_cache, len(cache), pieces[0], output_gate)
            cache.append(half)
        total = functools.reduce(jnp.add, [pieces[0]] + got)
    block = (kv_heads + 1) * steps * group
    tile = pl.pallas_call(
        functools.partial(attend_kernel, kv_heads, group, steps),
        out_shape=struct((block, head_size), BF16),
        in_specs=[VMEM] * 7,
        out_specs=VMEM,
        scratch_shapes=[
            pltpu.SMEM(image_first_slot.shape, jnp.int32),
            pltpu.SMEM(tile_count.shape, jnp.int32),
            pltpu.SMEM(cross_tile_mask.shape, jnp.int32),
            pltpu.SemaphoreType.DMA((3,)),
        ],
        compiler_params=params(6),
    )(total, query_gain, *cache, image_first_slot, tile_count, cross_tile_mask)
    stages = exchange_stages(devices.bit_length() - 1, [4, 3])
    order = positions(stages)
    gathered = tile[None]
    for group_bits in reversed(stages):
        gathered = jnp.concatenate(
            [gathered] + [exchange(gathered, step, devices) for step in offsets(group_bits)[1:]], axis=0
        )
    scratch = 4 * head_size * (2 * devices * steps * group + heads * rows * steps)
    return pl.pallas_call(
        functools.partial(finish_kernel, order, kv_heads, group, steps, cross_tile_mask.shape[2]),
        out_shape=struct((rows, steps, output_weight.shape[1]), BF16),
        in_specs=[VMEM] * 5,
        out_specs=VMEM,
        scratch_shapes=[
            pltpu.VMEM((2, devices * steps * group, head_size), F32),
            pltpu.VMEM((heads * rows * steps, head_size), F32),
        ],
        compiler_params=params(6 + (2 * scratch >> 20)),
    )(gate, image_first_slot, tile_count, gathered, output_weight)


def solution(mesh):
    return jax.shard_map(
        functools.partial(body, mesh.shape[AXIS]),
        mesh=mesh,
        in_specs=(
            P("groups", None, "tensor"),
            P("tensor", None),
            P(),
            P(("groups", "tensor"), None, None),
            P("groups"),
            P("groups"),
            P("groups", None, None),
            P(None, "tensor"),
            P(),
        ),
        out_specs=P("groups", None, "tensor"),
        check_vma=False,
    )
```
